256 devices in a mesh: ctx: 64 (over y, x_hi, z), head: 4 (over x_lo, core).
Axes of the slice: x: 4 (x_hi: 2, x_lo: 2; x = x_hi * 2 + x_lo), y: 4, z: 8, core: 2. Of those that a mesh axis runs over, the one named last changes fastest.
Arguments:
- queries: bfloat16 [65536, 2048], P('ctx', 'head'), may hold values from -12 to 12
- keys: bfloat16 [65536, 2048], P('ctx', 'head'), may hold values from -12 to 12
- values: bfloat16 [65536, 2048], P('ctx', 'head'), may hold values from -40 to 40
- norm_gain: float32 [2048], P('head'), may hold values from 0.1 to 1.9
Outputs:
- normed: bfloat16 [65536, 2048], P('ctx', 'head')
The draws below stay inside these ranges and needn't reach their ends.
All inputs are finite; a program needn't handle non-finite values.
Results may differ from the reference program's by a relative error of at most 0.025.
Values may be sent and summed in bfloat16 or wider, within the bound.
No kernel may reach another device: no remote copies, remote signals or barrier semaphores. Data moves between devices by JAX's collectives and lax.ppermute only.
A program may use at most 128 MiB of HBM per device.

```python
import math
import jax
import jax.numpy as jnp
from jax import lax

HEADS = 16
HEAD_DIM = 128
BLOCK = 128
FEAT = 2048
SEQ = 65536


def draw_queries(key, part):
    key = jax.random.fold_in(key, 1)
    return jnp.clip(jax.random.normal(key, (SEQ, FEAT), jnp.float32), -6.0, 6.0).astype(jnp.bfloat16)


def draw_keys(key, part):
    key = jax.random.fold_in(key, 2)
    return jnp.clip(jax.random.normal(key, (SEQ, FEAT), jnp.float32), -6.0, 6.0).astype(jnp.bfloat16)


def draw_values(key, part):
    key = jax.random.fold_in(key, 3)
    heads = (jnp.arange(FEAT) // HEAD_DIM).astype(jnp.float32)
    rising = 10.0 ** (heads / (HEADS - 1))
    fresh = jnp.clip(jax.random.normal(key, (SEQ, FEAT), jnp.float32), -4.0, 4.0)
    return (fresh * rising).astype(jnp.bfloat16)


def setup_inputs(seed: int = 0) -> dict:
    splits = jax.random.split(jax.random.key(seed), 5)
    return {
        "queries": draw_queries(jax.random.fold_in(splits[4], 71), 0),
        "keys": draw_keys(jax.random.fold_in(splits[4], 71), 0),
        "values": draw_values(jax.random.fold_in(splits[4], 71), 0),
        "norm_gain": jnp.clip(1.0 + 0.18 * jax.random.normal(splits[3], (FEAT,), jnp.float32), 0.1, 1.9),
    }


def coarsen(rows):
    halves = rows.astype(jnp.float32).reshape(rows.shape[0] // 2, 2, rows.shape[1])
    return ((halves[:, 0] + halves[:, 1]) * 0.5).astype(jnp.bfloat16)

def group_terms(front, keyset, valueset):
    scale = 1.0 / math.sqrt(front.shape[-1])
    scores = jnp.einsum('gqhe,gkhe->ghqk', front.astype(jnp.float32), keyset.astype(jnp.float32)) * scale
    top = lax.optimization_barrier(jnp.max(scores, axis=-1))
    weights = jnp.exp(scores - top[..., None]).astype(jnp.bfloat16)
    numer = jnp.einsum('ghqk,gkhe->gqhe', weights.astype(jnp.float32), valueset.astype(jnp.float32))
    denom = lax.optimization_barrier(jnp.sum(weights.astype(jnp.float32), axis=-1))
    return (jnp.swapaxes(top, 1, 2), numer, jnp.swapaxes(denom, 1, 2))

def level_terms(front, keyset, valueset):
    groups = front.shape[0]
    batch = min(groups, 8)

    def one_batch(items):
        return group_terms(items[0], items[1], items[2])
    shaped = tuple((a.reshape((groups // batch, batch) + a.shape[1:]) for a in (front, keyset, valueset)))
    top, numer, denom = lax.map(one_batch, shaped)
    count = groups * front.shape[1]
    return (top.reshape(count, HEADS), numer.reshape(count, HEADS, HEAD_DIM), denom.reshape(count, HEADS))

def sibling_blocks(block):
    count = block.shape[0] // BLOCK
    paired = block.reshape(count // 2, 2, BLOCK, HEADS, HEAD_DIM)[:, ::-1]
    return paired.reshape(count, BLOCK, HEADS, HEAD_DIM)

def merge_in(state, terms, weight):
    if state is None:
        return (terms[0], terms[1] * weight, terms[2] * weight)
    top = jnp.maximum(state[0], terms[0])
    older = jnp.exp(state[0] - top)
    newer = jnp.exp(terms[0] - top) * weight
    return (top, state[1] * older[..., None] + terms[1] * newer[..., None], state[2] * older + terms[2] * newer)

def widen(state):
    return tuple((jnp.repeat(a, 2, axis=0) for a in state))

def reference(queries, keys, values, norm_gain):
    levels = (SEQ // BLOCK).bit_length() - 1
    fronts = [queries]
    key_rows = [keys]
    value_rows = [values]
    for level in range(1, levels):
        fronts.append(coarsen(fronts[-1]))
        key_rows.append(coarsen(key_rows[-1]))
        value_rows.append(coarsen(value_rows[-1]))
    state = None
    for level in range(levels - 1, -1, -1):
        count = fronts[level].shape[0]
        if level == 0:
            size = 2 * BLOCK
            front = fronts[0].reshape(count // size, size, HEADS, HEAD_DIM)
            keyset = key_rows[0].reshape(count // size, size, HEADS, HEAD_DIM)
            valueset = value_rows[0].reshape(count // size, size, HEADS, HEAD_DIM)
        else:
            front = fronts[level].reshape(count // BLOCK, BLOCK, HEADS, HEAD_DIM)
            keyset = sibling_blocks(key_rows[level])
            valueset = sibling_blocks(value_rows[level])
        terms = level_terms(front, keyset, valueset)
        if state is not None:
            state = widen(state)
        state = merge_in(state, terms, 2.0 ** level)
    attention = (state[1] / state[2][..., None]).reshape(SEQ, FEAT)
    meansq = lax.optimization_barrier(jnp.mean(attention * attention, axis=-1, keepdims=True))
    return (attention * lax.rsqrt(meansq + 1e-06) * norm_gain).astype(jnp.bfloat16)
```

```python
import functools
import math

import jax
import jax.numpy as jnp
import numpy as np
from jax import lax
from jax.experimental import pallas as pl
from jax.experimental.pallas import tpu as pltpu
from jax.sharding import PartitionSpec as P

HEAD_DIM = 128
BLOCK = 128
FEAT = 2048
HEADS = 4
ROWS = 1024
WIDTH = HEADS * HEAD_DIM
GROUP = 256
GROUPS = ROWS // GROUP
SLABS = GROUP // 8
SCALE = math.log2(math.e) / math.sqrt(HEAD_DIM)
BF16 = jnp.bfloat16
F32 = jnp.float32
VMEM_LIMIT = 48 * 1024 * 1024


def slab_order():
    token = np.arange(GROUP)
    return token // 128 * 128 + token % 16 * 8 + token // 16 % 8


def order_matrix():
    matrix = np.zeros((GROUP, GROUP), np.float32)
    matrix[slab_order(), np.arange(GROUP)] = 1.0
    return jnp.asarray(matrix, BF16)


def first_means():
    token = np.arange(GROUP)
    matrix = np.zeros((GROUP // 2, GROUP), np.float32)
    matrix[token // 128 * 64 + token % 16 // 2 * 8 + token // 16 % 8, token] = 0.5
    return jnp.asarray(matrix, BF16)


def pair_means(rows):
    matrix = np.zeros((rows // 2, rows), np.float32)
    matrix[np.arange(rows) // 2, np.arange(rows)] = 0.5
    return jnp.asarray(matrix, BF16)


def slab_pair_means(rows):
    row = np.arange(rows)
    matrix = np.zeros((rows // 2, rows), np.float32)
    matrix[row // 16 * 8 + row % 8, row] = 0.5
    return jnp.asarray(matrix, BF16)


def spread_means():
    rows = np.arange(64)
    out = []
    for step in range(4):
        matrix = np.zeros((64, 64), np.float32)
        base = rows >> (step + 1) << (step + 1)
        matrix[rows, base] = 0.5
        matrix[rows, base + (1 << step)] = 0.5
        out.append(matrix)
    return jnp.asarray(np.concatenate(out), BF16)


def dot(a, b):
    return jnp.dot(a, b, preferred_element_type=F32)


def slab_means(x):
    rows, width = x.shape
    x = x.reshape(rows // 16, 2, 8, width)
    return ((x[:, 0] + x[:, 1]) * 0.5).reshape(rows // 2, width)


def rounded_slab_means(x):
    return slab_means(x.astype(F32)).astype(BF16)


def attend(front, keyset, valueset):
    scores = lax.dot_general(front, keyset, (((1,), (1,)), ((), ())), preferred_element_type=F32)
    top = jnp.max(scores, axis=-1, keepdims=True)
    weights = jnp.exp2((scores - top) * SCALE).astype(BF16)
    both = jnp.concatenate([valueset, jnp.ones(valueset.shape, BF16)], axis=1)
    sums = dot(weights, both)
    return jnp.broadcast_to(top * SCALE, (front.shape[0], HEAD_DIM)), sums[:, :HEAD_DIM], sums[:, HEAD_DIM:]


def join(parts):
    top = functools.reduce(jnp.maximum, [part[0] for part in parts])
    numer = denom = None
    for (peak, n, d), level in parts_with(parts):
        factor = jnp.exp2(peak - top + level)
        numer = n * factor if numer is None else numer + n * factor
        denom = d * factor if denom is None else denom + d * factor
    return top, numer, denom


def parts_with(parts):
    return [(part[:3], part[3]) for part in parts]


def spread(x, copies):
    rows, width = x.shape
    x = jnp.broadcast_to(x.reshape(rows // 8, 1, 8, width), (rows // 8, copies, 8, width))
    return x.reshape(rows * copies, width)


def coarse_kernel(means_ref, k_ref, v_ref, out_ref):
    for which, ref in enumerate((k_ref, v_ref)):
        x = dot(means_ref[...], ref[...]).astype(BF16)
        x = rounded_slab_means(rounded_slab_means(x))
        out_ref[which] = x


def coarse(k, v):
    spec = pl.BlockSpec((GROUP, WIDTH), lambda g: (g, 0))
    return pl.pallas_call(
        coarse_kernel,
        grid=(GROUPS,),
        in_specs=[pl.BlockSpec((GROUP // 2, GROUP), lambda g: (0, 0)), spec, spec],
        out_specs=pl.BlockSpec((2, GROUP // 8, WIDTH), lambda g: (0, g, 0)),
        out_shape=jax.ShapeDtypeStruct((2, BLOCK, WIDTH), BF16),
        cost_estimate=pl.CostEstimate(flops=3 * 10**8, bytes_accessed=2 * 2**20, transcendentals=0),
        compiler_params=pltpu.CompilerParams(vmem_limit_bytes=VMEM_LIMIT),
        name="coarse",
    )(first_means(), k, v)


def step_kernel(means_ref, own_ref, far_ref, out_ref):
    for which in range(2):
        out_ref[which, : BLOCK // 2] = dot(means_ref[...], own_ref[which]).astype(BF16)
        out_ref[which, BLOCK // 2 :] = dot(means_ref[...], far_ref[which]).astype(BF16)


def step(means, own, far):
    return pl.pallas_call(
        step_kernel,
        out_shape=jax.ShapeDtypeStruct((2, BLOCK, WIDTH), BF16),
        cost_estimate=pl.CostEstimate(flops=10**8, bytes_accessed=2**20, transcendentals=0),
        compiler_params=pltpu.CompilerParams(vmem_limit_bytes=VMEM_LIMIT),
        name="coarse_step",
    )(means, own, far)


def local_kernel(order_ref, means_ref, spread_ref, q_ref, k_ref, v_ref, att_ref, lse_ref, q3_ref, qx_ref):
    lane = lax.broadcasted_iota(jnp.int32, (SLABS, 8, HEAD_DIM), 2)
    slab = lax.broadcasted_iota(jnp.int32, (SLABS, 8, HEAD_DIM), 0)
    groups = range(GROUPS)
    rows = [slice(GROUP * g, GROUP * (g + 1)) for g in groups]
    q0, q1, q2, kv1, kv2 = [], [], [], [], []
    for g in groups:
        front = dot(order_ref[...], q_ref[rows[g], :])
        q0.append(front.astype(BF16))
        q1.append(slab_means(front).astype(BF16))
        q2.append(rounded_slab_means(q1[g]))
        both = jnp.concatenate([k_ref[rows[g], :], v_ref[rows[g], :]], axis=1)
        kv1.append(dot(means_ref[...], both).astype(BF16))
        kv2.append(rounded_slab_means(kv1[g]))
    q3 = rounded_slab_means(jnp.concatenate(q2, axis=0))
    q3_ref[...] = q3
    front = rounded_slab_means(q3)
    qx_ref[0:64, :] = front
    for i in range(4):
        front = dot(spread_ref[64 * i : 64 * (i + 1), :], front).astype(BF16)
        qx_ref[64 * (i + 1) : 64 * (i + 2), :] = front
    second = []
    for pair in range(2):
        far = jnp.concatenate(kv2[2 - 2 * pair : 4 - 2 * pair], axis=0)
        front = jnp.concatenate(q2[2 * pair : 2 * pair + 2], axis=0)
        second.append(attend(front, far[:, :HEAD_DIM], far[:, HEAD_DIM:]))
    for g in groups:
        part0 = attend(q0[g], k_ref[rows[g], :], v_ref[rows[g], :])
        far = kv1[g ^ 1]
        part1 = attend(q1[g], far[:, :HEAD_DIM], far[:, HEAD_DIM:])
        half = slice(64 * (g % 2), 64 * (g % 2 + 1))
        part2 = [x[half] for x in second[g // 2]]
        top, numer, denom = join(
            [
                (*part0, 0.0),
                (*[spread(x, 2) for x in part1], 1.0),
                (*[spread(x, 4) for x in part2], 2.0),
            ]
        )
        att_ref[rows[g], :] = numer / denom
        lse = (top + jnp.log2(denom)).reshape(SLABS, 8, HEAD_DIM)
        lse_ref[0, g] = jnp.sum(jnp.where(lane == slab, lse, 0.0), axis=0)


def local(q, k, v):
    column = pl.BlockSpec((ROWS, HEAD_DIM), lambda h: (0, h))
    return pl.pallas_call(
        local_kernel,
        grid=(HEADS,),
        in_specs=[
            pl.BlockSpec((GROUP, GROUP), lambda h: (0, 0)),
            pl.BlockSpec((GROUP // 2, GROUP), lambda h: (0, 0)),
            pl.BlockSpec((256, 64), lambda h: (0, 0)),
            column,
            column,
            column,
        ],
        out_specs=[
            column,
            pl.BlockSpec((1, GROUPS, 8, 128), lambda h: (h, 0, 0, 0)),
            pl.BlockSpec((BLOCK, HEAD_DIM), lambda h: (0, h)),
            pl.BlockSpec((320, HEAD_DIM), lambda h: (0, h)),
        ],
        out_shape=[
            jax.ShapeDtypeStruct((ROWS, WIDTH), F32),
            jax.ShapeDtypeStruct((HEADS, GROUPS, 8, 128), F32),
            jax.ShapeDtypeStruct((BLOCK, WIDTH), BF16),
            jax.ShapeDtypeStruct((320, WIDTH), BF16),
        ],
        cost_estimate=pl.CostEstimate(flops=3 * 10**9, bytes_accessed=6 * 2**20, transcendentals=2 * 10**6),
        compiler_params=pltpu.CompilerParams(vmem_limit_bytes=VMEM_LIMIT),
        name="local_levels",
    )(order_matrix(), first_means(), spread_means(), q, k, v)


def far_kernel(q3_ref, qx_ref, *refs):
    fars, (att_ref, lse_ref) = refs[:-2], refs[-2:]
    for h in range(HEADS):
        col = slice(HEAD_DIM * h, HEAD_DIM * (h + 1))
        part3 = attend(q3_ref[:, col], fars[0][0, :, col], fars[0][1, :, col])
        parts = []
        for i, far in enumerate(fars[1:]):
            got = attend(qx_ref[64 * i : 64 * (i + 1), col], far[0, :, col], far[1, :, col])
            parts.append((*[spread(x, 2) for x in got], 4.0 + i))
        top, numer, denom = join([(*part3, 3.0)] + parts)
        att_ref[:, col] = numer / denom
        lse_ref[:, col] = top + jnp.log2(denom)


def far_levels(q3, qx, fars):
    return pl.pallas_call(
        far_kernel,
        out_shape=[jax.ShapeDtypeStruct((BLOCK, WIDTH), F32)] * 2,
        cost_estimate=pl.CostEstimate(flops=10**9, bytes_accessed=2 * 2**20, transcendentals=3 * 10**5),
        compiler_params=pltpu.CompilerParams(vmem_limit_bytes=VMEM_LIMIT),
        name="far_levels",
    )(q3, qx, *fars)


def merge_kernel(qx_ref, last_ref, fatt_ref, flse_ref, att_ref, lse_ref, out_ref, ss_ref, state, peaks):
    g = pl.program_id(0)

    @pl.when(g == 0)
    def _():
        ss_ref[...] = jnp.zeros(ss_ref.shape, F32)
        for h in range(HEADS):
            col = slice(HEAD_DIM * h, HEAD_DIM * (h + 1))
            top, numer, denom = attend(qx_ref[:, col], last_ref[0, :, col], last_ref[1, :, col])
            mean = spread(numer / denom, 2)
            peak = spread(top + jnp.log2(denom) + 8.0, 2)
            share = 1.0 / (1.0 + jnp.exp2(peak - flse_ref[:, col]))
            state[:, col] = mean + share * (fatt_ref[:, col] - mean)
            most = jnp.maximum(peak, flse_ref[:, col])
            peaks[:, col] = most + jnp.log2(jnp.exp2(peak - most) + jnp.exp2(flse_ref[:, col] - most))

    lane = lax.broadcasted_iota(jnp.int32, (8, 128), 1)
    shares = []
    fars = []
    start = pl.multiple_of(g * 32, 32)
    for h in range(HEADS):
        col = slice(HEAD_DIM * h, HEAD_DIM * (h + 1))
        peak = peaks[pl.ds(start, 32), col]
        far = jnp.zeros((8, 128), F32)
        for i in range(4):
            far = jnp.where(lane // 8 == i, peak[8 * i : 8 * (i + 1)], far)
        shares.append(1.0 / (1.0 + jnp.exp2(far - lse_ref[h, 0])))
        fars.append(state[pl.ds(start, 32), col])
    squares = jnp.zeros((8, 128), F32)
    for i in range(SLABS):
        rows = slice(8 * i, 8 * (i + 1))
        total = None
        for h in range(HEADS):
            col = slice(HEAD_DIM * h, HEAD_DIM * (h + 1))
            far = fars[h][8 * (i // 8) : 8 * (i // 8 + 1)]
            att = far + shares[h][:, i : i + 1] * (att_ref[rows, col] - far)
            out_ref[rows, col] = att
            total = att * att if total is None else total + att * att
        squares = jnp.where(lane == g * SLABS + i, jnp.sum(total, axis=1, keepdims=True), squares)
    ss_ref[...] += squares


def merge(qx, last, fatt, flse, att, lse):
    whole = lambda shape: pl.BlockSpec(shape, lambda g: (0,) * len(shape))
    rows = pl.BlockSpec((GROUP, WIDTH), lambda g: (g, 0))
    return pl.pallas_call(
        merge_kernel,
        grid=(GROUPS,),
        in_specs=[
            pl.BlockSpec((64, WIDTH), lambda g: (4, 0)),
            whole((2, BLOCK, WIDTH)),
            whole((BLOCK, WIDTH)),
            whole((BLOCK, WIDTH)),
            rows,
            pl.BlockSpec((HEADS, 1, 8, 128), lambda g: (0, g, 0, 0)),
        ],
        out_specs=[rows, whole((8, 128))],
        out_shape=[jax.ShapeDtypeStruct((ROWS, WIDTH), F32), jax.ShapeDtypeStruct((8, 128), F32)],
        scratch_shapes=[pltpu.VMEM((BLOCK, WIDTH), F32)] * 2,
        cost_estimate=pl.CostEstimate(flops=10**8, bytes_accessed=4 * 2**20, transcendentals=10**5),
        compiler_params=pltpu.CompilerParams(vmem_limit_bytes=VMEM_LIMIT),
        name="merge",
    )(qx, last, fatt, flse, att, lse)


def finish_kernel(back_ref, ss_ref, gain_ref, att_ref, out_ref):
    g = pl.program_id(0)
    lane = lax.broadcasted_iota(jnp.int32, (8, 128), 1)
    factor = lax.rsqrt(ss_ref[...] / FEAT + 1e-06)
    pieces = []
    for i in range(SLABS):
        one = jnp.sum(jnp.where(lane == g * SLABS + i, factor, 0.0), axis=1, keepdims=True)
        pieces.append(att_ref[8 * i : 8 * (i + 1), :] * one * gain_ref[...])
    normed = jnp.concatenate(pieces, axis=0).astype(BF16)
    out_ref[...] = dot(back_ref[...], normed).astype(BF16)


def finish(total, gain, att):
    rows = pl.BlockSpec((GROUP, WIDTH), lambda g: (g, 0))
    return pl.pallas_call(
        finish_kernel,
        grid=(GROUPS,),
        in_specs=[
            pl.BlockSpec((GROUP, GROUP), lambda g: (0, 0)),
            pl.BlockSpec((8, 128), lambda g: (0, 0)),
            pl.BlockSpec((1, WIDTH), lambda g: (0, 0)),
            rows,
        ],
        out_specs=rows,
        out_shape=jax.ShapeDtypeStruct((ROWS, WIDTH), BF16),
        cost_estimate=pl.CostEstimate(flops=3 * 10**8, bytes_accessed=3 * 2**20, transcendentals=0),
        compiler_params=pltpu.CompilerParams(vmem_limit_bytes=VMEM_LIMIT),
        name="finish",
    )(order_matrix().T, total, gain.reshape(1, WIDTH), att)


MASKS = (1, 3, 7, 8, 16, 48)


def body(queries, keys, values, norm_gain):
    count = lax.axis_size("ctx")
    own = coarse(keys, values)
    att, lse, q3, qx = local(queries, keys, values)
    fars = []
    for bit, mask in enumerate(MASKS):
        far = lax.ppermute(own, "ctx", [(i, i ^ mask) for i in range(count)])
        fars.append(far)
        if bit + 1 < len(MASKS):
            own = step(slab_pair_means(BLOCK) if bit == 0 else pair_means(BLOCK), own, far)
    fatt, flse = far_levels(q3, qx, fars[:-1])
    att, squares = merge(qx, fars[-1], fatt, flse, att, lse)
    total = lax.psum(squares, "head")
    return finish(total, norm_gain, att)


def solution(mesh):
    return jax.shard_map(
        body,
        mesh=mesh,
        in_specs=(P("ctx", "head"), P("ctx", "head"), P("ctx", "head"), P("head")),
        out_specs=P("ctx", "head"),
        check_vma=False,
    )
```

```python
import functools
import math

import jax
import jax.numpy as jnp
import numpy as np
from jax import lax
from jax.experimental import pallas as pl
from jax.experimental.pallas import tpu as pltpu
from jax.sharding import PartitionSpec as P

HEAD_DIM = 128
BLOCK = 128
FEAT = 2048
HEADS = 4
ROWS = 1024
WIDTH = HEADS * HEAD_DIM
HALF = WIDTH // 2
GROUP = 256
GROUPS = ROWS // GROUP
SLABS = GROUP // 8
SCALE = math.log2(math.e) / math.sqrt(HEAD_DIM)
BF16 = jnp.bfloat16
F32 = jnp.float32
VMEM_LIMIT = 48 * 1024 * 1024


def slab_order():
    token = np.arange(GROUP)
    return token // 128 * 128 + token % 16 * 8 + token // 16 % 8


def order_matrix():
    matrix = np.zeros((GROUP, GROUP), np.float32)
    matrix[slab_order(), np.arange(GROUP)] = 1.0
    return jnp.asarray(matrix, BF16)


def grid_of(rows, columns):
    row = lax.broadcasted_iota(jnp.int32, (rows, columns), 0)
    column = lax.broadcasted_iota(jnp.int32, (rows, columns), 1)
    return row, column


def halves(where):
    return jnp.where(where, 0.5, 0.0).astype(BF16)


def first_means():
    row, token = grid_of(GROUP // 2, GROUP)
    return halves(row == token // 128 * 64 + token % 16 // 2 * 8 + token // 16 % 8)


def pair_means(rows):
    row, column = grid_of(rows // 2, rows)
    return halves(column // 2 == row)


def spread_means(step):
    row, column = grid_of(64, 64)
    base = row // 2 ** (step + 1) * 2 ** (step + 1)
    return halves((column == base) | (column == base + 2**step))


def dot(a, b):
    return jnp.dot(a, b, preferred_element_type=F32)


def slab_means(x):
    rows, width = x.shape
    x = x.reshape(rows // 16, 2, 8, width)
    return ((x[:, 0] + x[:, 1]) * 0.5).reshape(rows // 2, width)


def rounded_slab_means(x):
    return slab_means(x.astype(F32)).astype(BF16)


def attend(front, keyset, valueset):
    scores = lax.dot_general(front, keyset, (((1,), (1,)), ((), ())), preferred_element_type=F32)
    top = jnp.max(scores, axis=-1, keepdims=True)
    weights = jnp.exp2((scores - top) * SCALE).astype(BF16)
    both = jnp.concatenate([valueset, jnp.ones(valueset.shape, BF16)], axis=1)
    sums = dot(weights, both)
    return jnp.broadcast_to(top * SCALE, (front.shape[0], HEAD_DIM)), sums[:, :HEAD_DIM], sums[:, HEAD_DIM:]


def join(parts):
    top = functools.reduce(jnp.maximum, [part[0] for part in parts])
    numer = denom = None
    for (peak, n, d), level in parts_with(parts):
        factor = jnp.exp2(peak - top + level)
        numer = n * factor if numer is None else numer + n * factor
        denom = d * factor if denom is None else denom + d * factor
    return top, numer, denom


def parts_with(parts):
    return [(part[:3], part[3]) for part in parts]


def spread(x, copies):
    rows, width = x.shape
    x = jnp.broadcast_to(x.reshape(rows // 8, 1, 8, width), (rows // 8, copies, 8, width))
    return x.reshape(rows * copies, width)


def my_half():
    z = lax.rem(lax.axis_index("ctx"), 8)
    return lax.rem(z + z // 2, 2)


def half_columns(half):
    return pl.ds(pl.multiple_of(half * HALF, HALF), HALF)


def params(limit=VMEM_LIMIT):
    return pltpu.CompilerParams(vmem_limit_bytes=limit)


def cost(flops, bytes_accessed):
    return pl.CostEstimate(flops=flops, bytes_accessed=bytes_accessed, transcendentals=0)


def coarse_kernel(x_ref, held_ref, third_ref, own_ref, send_ref, fourth, sems):
    copies = []
    for g in range(GROUPS):
        rows = pl.ds(GROUP * g, GROUP)
        copy = pltpu.make_async_copy(x_ref.at[rows], held_ref.at[rows], sems.at[g])
        copy.start()
        copies.append(copy)
    means = first_means()
    for g in range(GROUPS):
        copies[g].wait()
        x = dot(means, held_ref[GROUP * g : GROUP * (g + 1), :]).astype(BF16)
        x = rounded_slab_means(rounded_slab_means(x))
        third_ref[32 * g : 32 * (g + 1), :] = x
        fourth[16 * g : 16 * (g + 1), :] = rounded_slab_means(x)
    half = my_half()
    own_ref[...] = fourth[:, half_columns(half)]
    send_ref[...] = fourth[:, half_columns(1 - half)]


def coarse(x):
    return pl.pallas_call(
        coarse_kernel,
        in_specs=[pl.BlockSpec(memory_space=pl.ANY)],
        out_shape=[
            pltpu.VMEM((ROWS, WIDTH), BF16),
            pltpu.VMEM((BLOCK, WIDTH), BF16),
            pltpu.VMEM((64, HALF), BF16),
            pltpu.VMEM((64, HALF), BF16),
        ],
        scratch_shapes=[pltpu.VMEM((64, WIDTH), BF16), pltpu.SemaphoreType.DMA((GROUPS,))],
        cost_estimate=cost(2 * 10**8, 2**20),
        compiler_params=params(),
        name="coarse",
    )(pltpu.with_memory_space_constraint(x, pltpu.HBM))


def stack_kernel(own_ref, far_ref, out_ref):
    out_ref[:64] = own_ref[...]
    out_ref[64:] = far_ref[...]


def step_kernel(own_ref, far_ref, out_ref):
    means = pair_means(BLOCK)
    out_ref[:64] = dot(means, own_ref[...]).astype(BF16)
    out_ref[64:] = dot(means, far_ref[...]).astype(BF16)


def next_block(kernel, own, far):
    return pl.pallas_call(
        kernel,
        out_shape=jax.ShapeDtypeStruct((BLOCK, HALF), BF16),
        cost_estimate=cost(10**8, 2**18),
        compiler_params=params(),
        name="next_block",
    )(own, far)


def next_fronts(front):
    out = [front]
    for i in range(4):
        out.append(dot(spread_means(i), out[-1]).astype(BF16))
    return out


def local_kernel(first, order_ref, q_ref, k_ref, v_ref, att_ref, lse_ref, q3_ref, qx_ref):
    lane = lax.broadcasted_iota(jnp.int32, (SLABS, 8, HEAD_DIM), 2)
    slab = lax.broadcasted_iota(jnp.int32, (SLABS, 8, HEAD_DIM), 0)
    groups = range(GROUPS)
    rows = [slice(GROUP * g, GROUP * (g + 1)) for g in groups]
    means = first_means()

    def one_head(h, carry):
        into = pl.ds(pl.multiple_of(h * HEAD_DIM, HEAD_DIM), HEAD_DIM)
        col = pl.ds(pl.multiple_of((h + first) * HEAD_DIM, HEAD_DIM), HEAD_DIM)
        q0, q1, q2, kv1, kv2 = [], [], [], [], []
        for g in groups:
            front = dot(order_ref[...], q_ref[rows[g], col])
            q0.append(front.astype(BF16))
            q1.append(slab_means(front).astype(BF16))
            q2.append(rounded_slab_means(q1[g]))
            both = jnp.concatenate([k_ref[rows[g], col], v_ref[rows[g], col]], axis=1)
            kv1.append(dot(means, both).astype(BF16))
            kv2.append(rounded_slab_means(kv1[g]))
        q3 = rounded_slab_means(jnp.concatenate(q2, axis=0))
        q3_ref[:, into] = q3
        for i, front in enumerate(next_fronts(rounded_slab_means(q3))):
            qx_ref[64 * i : 64 * (i + 1), into] = front
        second = []
        for pair in range(2):
            far = jnp.concatenate(kv2[2 - 2 * pair : 4 - 2 * pair], axis=0)
            front = jnp.concatenate(q2[2 * pair : 2 * pair + 2], axis=0)
            second.append(attend(front, far[:, :HEAD_DIM], far[:, HEAD_DIM:]))
        for g in groups:
            part0 = attend(q0[g], k_ref[rows[g], col], v_ref[rows[g], col])
            far = kv1[g ^ 1]
            part1 = attend(q1[g], far[:, :HEAD_DIM], far[:, HEAD_DIM:])
            half = slice(64 * (g % 2), 64 * (g % 2 + 1))
            part2 = [x[half] for x in second[g // 2]]
            top, numer, denom = join(
                [
                    (*part0, 0.0),
                    (*[spread(x, 2) for x in part1], 1.0),
                    (*[spread(x, 4) for x in part2], 2.0),
                ]
            )
            att_ref[rows[g], into] = numer / denom
            lse = (top + jnp.log2(denom)).reshape(SLABS, 8, HEAD_DIM)
            lse_ref[h, g] = jnp.sum(jnp.where(lane == slab, lse, 0.0), axis=0)
        return carry

    lax.fori_loop(0, 2, one_head, 0)


def local(first, q, k, v):
    return pl.pallas_call(
        functools.partial(local_kernel, first),
        out_shape=[
            jax.ShapeDtypeStruct((ROWS, HALF), F32),
            jax.ShapeDtypeStruct((2, GROUPS, 8, 128), F32),
            jax.ShapeDtypeStruct((BLOCK, HALF), BF16),
            jax.ShapeDtypeStruct((320, HALF), BF16),
        ],
        cost_estimate=cost(3 * 10**9, 3 * 2**20),
        compiler_params=params(),
        name="local_levels",
    )(order_matrix(), q, k, v)


def pack_kernel(k3_ref, v3_ref, qa_ref, qb_ref, out_ref):
    out_ref[0:128] = k3_ref[...]
    out_ref[128:256] = v3_ref[...]
    half = my_half()

    @pl.when(half == 1)
    def _():
        out_ref[256:288, :HALF] = qa_ref[0:32]
        out_ref[256:288, HALF:] = qa_ref[32:64]

    @pl.when(half == 0)
    def _():
        out_ref[256:288, :HALF] = qb_ref[0:32]
        out_ref[256:288, HALF:] = qb_ref[32:64]


def pack(k3, v3, qxs):
    return pl.pallas_call(
        pack_kernel,
        out_shape=jax.ShapeDtypeStruct((288, WIDTH), BF16),
        cost_estimate=cost(10, 2**19),
        compiler_params=params(),
        name="pack",
    )(k3, v3, *qxs)


def slab_lanes(x, copies):
    count = x.shape[0] // 8
    lane = lax.broadcasted_iota(jnp.int32, (count, 8, HEAD_DIM), 2)
    slab = lax.broadcasted_iota(jnp.int32, (count, 8, HEAD_DIM), 0)
    return jnp.sum(jnp.where(lane // copies == slab, x.reshape(count, 8, HEAD_DIM), 0.0), axis=0)


def third_kernel(near_ref, q3a_ref, q3b_ref, att_ref, lse_ref):
    for h in range(HEADS):
        col = slice(HEAD_DIM * h, HEAD_DIM * (h + 1))
        q3 = (q3a_ref, q3b_ref)[h // 2][:, HEAD_DIM * (h % 2) : HEAD_DIM * (h % 2 + 1)]
        top, numer, denom = attend(q3, near_ref[0:128, col], near_ref[128:256, col])
        att_ref[:, col] = numer / denom
        lse_ref[h] = slab_lanes(top + jnp.log2(denom) + 3.0, 1)


def third(near, q3s):
    return pl.pallas_call(
        third_kernel,
        out_shape=[jax.ShapeDtypeStruct((BLOCK, WIDTH), F32), jax.ShapeDtypeStruct((HEADS, 8, 128), F32)],
        cost_estimate=cost(10**8, 2**19),
        compiler_params=params(),
        name="third_level",
    )(near, *q3s)


def far_kernel(near_ref, qa_ref, qb_ref, *refs):
    fars, (att_ref, lse_ref, q8_ref, fronts) = refs[:-4], refs[-4:]
    half = my_half()

    @pl.when(half == 0)
    def _():
        fronts[...] = qa_ref[...]

    @pl.when(half == 1)
    def _():
        fronts[...] = qb_ref[...]

    theirs = next_fronts(jnp.concatenate([near_ref[256:288, :HALF], near_ref[256:288, HALF:]], axis=0))
    both = [jnp.concatenate([fronts[64 * i : 64 * (i + 1)], theirs[i]], axis=0) for i in range(5)]
    q8_ref[...] = both[4]
    for h in range(2):
        col = slice(HEAD_DIM * h, HEAD_DIM * (h + 1))
        parts = []
        for i in range(4):
            got = attend(both[i][:, col], fars[2 * i][:, col], fars[2 * i + 1][:, col])
            parts.append((*got, 4.0 + i))
        top, numer, denom = join(parts)
        att_ref[:, col] = numer / denom
        lse_ref[:, col] = top + jnp.log2(denom)


def far_levels(near, qxs, fars):
    return pl.pallas_call(
        far_kernel,
        out_shape=[
            jax.ShapeDtypeStruct((BLOCK, HALF), F32),
            jax.ShapeDtypeStruct((BLOCK, HALF), F32),
            jax.ShapeDtypeStruct((BLOCK, HALF), BF16),
        ],
        scratch_shapes=[pltpu.VMEM((320, HALF), BF16)],
        cost_estimate=cost(5 * 10**8, 2**20),
        compiler_params=params(),
        name="far_levels",
    )(near, *qxs, *fars)


def last_kernel(q8_ref, k_ref, v_ref, att_ref, lse_ref, own_ref, send_ref):
    for h in range(2):
        col = slice(HEAD_DIM * h, HEAD_DIM * (h + 1))
        top, numer, denom = attend(q8_ref[:, col], k_ref[:, col], v_ref[:, col])
        mean = numer / denom
        peak = top + jnp.log2(denom) + 8.0
        old = lse_ref[:, col]
        share = 1.0 / (1.0 + jnp.exp2(peak - old))
        att = mean + share * (att_ref[:, col] - mean)
        most = jnp.maximum(peak, old)
        peak = most + jnp.log2(jnp.exp2(peak - most) + jnp.exp2(old - most))
        for ref, rows in ((own_ref, slice(0, 64)), (send_ref, slice(64, 128))):
            ref[0:64, col] = att[rows]
            ref[64:72, col] = slab_lanes(peak[rows], 2)


def last_level(q8, k, v, att, lse):
    return pl.pallas_call(
        last_kernel,
        out_shape=[jax.ShapeDtypeStruct((72, HALF), F32)] * 2,
        cost_estimate=cost(10**8, 2**18),
        compiler_params=params(),
        name="last_level",
    )(q8, k, v, att, lse)


def merge_kernel(own_ref, got_ref, att3_ref, lse3_ref, atta_ref, attb_ref, lsea_ref, lseb_ref, out_ref, ss_ref, far):
    half = my_half()
    far[:, half_columns(half)] = own_ref[...]
    far[:, half_columns(1 - half)] = got_ref[...]
    lane = lax.broadcasted_iota(jnp.int32, (8, 128), 1)
    means, shares = [], []
    for h in range(HEADS):
        col = slice(HEAD_DIM * h, HEAD_DIM * (h + 1))
        peak, old = far[64:72, col], lse3_ref[h]
        share = 1.0 / (1.0 + jnp.exp2(peak - old))
        rows = []
        for n in range(16):
            mean = far[8 * (n // 2) : 8 * (n // 2 + 1), col]
            rows.append(mean + share[:, n : n + 1] * (att3_ref[8 * n : 8 * (n + 1), col] - mean))
        means.append(rows)
        most = jnp.maximum(peak, old)
        peak = most + jnp.log2(jnp.exp2(peak - most) + jnp.exp2(old - most))
        row = []
        for g in range(GROUPS):
            other = jnp.zeros((8, 128), F32)
            for i in range(4):
                other = jnp.where(lane // 8 == i, peak[:, 4 * g + i : 4 * g + i + 1], other)
            row.append(1.0 / (1.0 + jnp.exp2(other - (lsea_ref, lseb_ref)[h // 2][h % 2, g])))
        shares.append(row)
    ones = jnp.ones((HEAD_DIM, HEAD_DIM), BF16)
    squares = jnp.zeros((8, 128), F32)
    for g in range(GROUPS):
        totals = []
        for i in range(SLABS):
            rows = slice(GROUP * g + 8 * i, GROUP * g + 8 * (i + 1))
            total = None
            for h in range(HEADS):
                near_ref = (atta_ref, attb_ref)[h // 2]
                near = near_ref[rows, HEAD_DIM * (h % 2) : HEAD_DIM * (h % 2 + 1)]
                mean = means[h][4 * g + i // 8]
                att = mean + shares[h][g][:, i : i + 1] * (near - mean)
                out_ref[rows, HEAD_DIM * h : HEAD_DIM * (h + 1)] = att
                total = att * att if total is None else total + att * att
            totals.append(total)
        total = jnp.concatenate(totals, axis=0)
        high = total.astype(BF16)
        low = (total - high.astype(F32)).astype(BF16)
        total = dot(high, ones) + dot(low, ones)
        for i in range(SLABS):
            squares = jnp.where(lane == g * SLABS + i, total[8 * i : 8 * (i + 1)], squares)
    ss_ref[...] = squares


def merge(*args):
    return pl.pallas_call(
        merge_kernel,
        out_shape=[jax.ShapeDtypeStruct((ROWS, WIDTH), F32), jax.ShapeDtypeStruct((8, 128), F32)],
        scratch_shapes=[pltpu.VMEM((72, WIDTH), F32)],
        cost_estimate=cost(10**8, 4 * 2**20),
        compiler_params=params(),
        name="merge",
    )(*args)


def finish_kernel(back_ref, ss_ref, gain_ref, att_ref, out_ref, held, sems):
    factor = lax.rsqrt(ss_ref[...] / FEAT + 1e-06)
    copies = []
    for g in range(GROUPS):
        pieces = []
        for i in range(SLABS):
            n = g * SLABS + i
            pieces.append(att_ref[8 * n : 8 * (n + 1), :] * factor[:, n : n + 1] * gain_ref[...])
        normed = jnp.concatenate(pieces, axis=0).astype(BF16)
        held[g] = dot(back_ref[...], normed).astype(BF16)
        copy = pltpu.make_async_copy(held.at[g], out_ref.at[pl.ds(GROUP * g, GROUP)], sems.at[g])
        copy.start()
        copies.append(copy)
    for copy in copies:
        copy.wait()


def finish(total, gain, att):
    return pl.pallas_call(
        finish_kernel,
        out_specs=pl.BlockSpec(memory_space=pl.ANY),
        out_shape=jax.ShapeDtypeStruct((ROWS, WIDTH), BF16),
        scratch_shapes=[pltpu.VMEM((GROUPS, GROUP, WIDTH), BF16), pltpu.SemaphoreType.DMA((GROUPS,))],
        cost_estimate=pl.CostEstimate(flops=3 * 10**8, bytes_accessed=3 * 2**20, transcendentals=0),
        compiler_params=pltpu.CompilerParams(vmem_limit_bytes=VMEM_LIMIT),
        name="finish",
    )(order_matrix().T, total, gain.reshape(1, WIDTH), att)


MASKS = (3, 7, 8, 16, 48)


def after(args, *others):
    return lax.optimization_barrier((args, others))[0]


def body(queries, keys, values, norm_gain):
    count = lax.axis_size("ctx")

    def swap(x, mask):
        return lax.ppermute(x, "ctx", [(i, i ^ mask) for i in range(count)])

    held_k, k3, own_k, send_k = coarse(keys)
    held_v, v3, own_v, send_v = coarse(after(values, send_k))
    queries = after(queries, send_v)
    far = [swap(send_k, 1), swap(send_v, 1)]
    own = [next_block(stack_kernel, a, b) for a, b in zip((own_k, own_v), far)]
    locals_ = []
    fars = []
    near = None
    for bit, mask in enumerate(MASKS):
        far = [swap(x, mask) for x in own]
        if bit < 2:
            got = local(2 * bit, *after((queries, held_k, held_v), own))
            got, far = lax.optimization_barrier((got, far))
            locals_.append(got)
        if bit == 2:
            qxs = [x[3] for x in locals_]
            near = swap(pack(k3, v3, qxs), 1)
        fars += far
        if bit + 1 < len(MASKS):
            own = [next_block(step_kernel, a, b) for a, b in zip(own, far)]
    att7, lse7, q8 = far_levels(near, qxs, fars[:-2])
    kept, sent = last_level(q8, fars[-2], fars[-1], att7, lse7)
    got = swap(sent, 1)
    att3, lse3 = third(near, [x[2] for x in locals_])
    (atta, lsea), (attb, lseb) = [x[:2] for x in locals_]
    att, squares = merge(kept, got, att3, lse3, atta, attb, lsea, lseb)
    total = lax.psum(squares, "head")
    return finish(total, norm_gain, att)


def solution(mesh):
    return jax.shard_map(
        body,
        mesh=mesh,
        in_specs=(P("ctx", "head"), P("ctx", "head"), P("ctx", "head"), P("head")),
        out_specs=P("ctx", "head"),
        check_vma=False,
    )
```

```python
import functools
import math

import jax
import jax.numpy as jnp
import numpy as np
from jax import lax
from jax.experimental import pallas as pl
from jax.experimental.pallas import tpu as pltpu
from jax.sharding import PartitionSpec as P

HEAD_DIM = 128
BLOCK = 128
FEAT = 2048
HEADS = 4
ROWS = 1024
WIDTH = HEADS * HEAD_DIM
HALF = WIDTH // 2
GROUP = 256
GROUPS = ROWS // GROUP
SLABS = GROUP // 8
SCALE = math.log2(math.e) / math.sqrt(HEAD_DIM)
BF16 = jnp.bfloat16
F32 = jnp.float32
VMEM_LIMIT = 48 * 1024 * 1024


def slab_order():
    token = np.arange(GROUP)
    return token // 128 * 128 + token % 16 * 8 + token // 16 % 8


def order_matrix():
    matrix = np.zeros((GROUP, GROUP), np.float32)
    matrix[slab_order(), np.arange(GROUP)] = 1.0
    return jnp.asarray(matrix, BF16)


def grid_of(rows, columns):
    row = lax.broadcasted_iota(jnp.int32, (rows, columns), 0)
    column = lax.broadcasted_iota(jnp.int32, (rows, columns), 1)
    return row, column


def halves(where):
    return jnp.where(where, 0.5, 0.0).astype(BF16)


def first_means():
    row, token = grid_of(GROUP // 2, GROUP)
    return halves(row == token // 128 * 64 + token % 16 // 2 * 8 + token // 16 % 8)


def pair_means(rows):
    row, column = grid_of(rows // 2, rows)
    return halves(column // 2 == row)


def spread_means(step):
    row, column = grid_of(64, 64)
    base = row // 2 ** (step + 1) * 2 ** (step + 1)
    return halves((column == base) | (column == base + 2**step))


def dot(a, b):
    return jnp.dot(a, b, preferred_element_type=F32)


def slab_means(x):
    rows, width = x.shape
    x = x.reshape(rows // 16, 2, 8, width)
    return ((x[:, 0] + x[:, 1]) * 0.5).reshape(rows // 2, width)


def rounded_slab_means(x):
    return slab_means(x.astype(F32)).astype(BF16)


def attend(front, keyset, valueset):
    scores = lax.dot_general(front, keyset, (((1,), (1,)), ((), ())), preferred_element_type=F32)
    top = jnp.max(scores, axis=-1, keepdims=True)
    weights = jnp.exp2((scores - top) * SCALE).astype(BF16)
    both = jnp.concatenate([valueset, jnp.ones(valueset.shape, BF16)], axis=1)
    sums = dot(weights, both)
    return jnp.broadcast_to(top * SCALE, (front.shape[0], HEAD_DIM)), sums[:, :HEAD_DIM], sums[:, HEAD_DIM:]


def join(parts):
    top = functools.reduce(jnp.maximum, [part[0] for part in parts])
    numer = denom = None
    for (peak, n, d), level in parts_with(parts):
        factor = jnp.exp2(peak - top + level)
        numer = n * factor if numer is None else numer + n * factor
        denom = d * factor if denom is None else denom + d * factor
    return top, numer, denom


def parts_with(parts):
    return [(part[:3], part[3]) for part in parts]


def spread(x, copies):
    rows, width = x.shape
    x = jnp.broadcast_to(x.reshape(rows // 8, 1, 8, width), (rows // 8, copies, 8, width))
    return x.reshape(rows * copies, width)


def my_half():
    return lax.rem(lax.axis_index("ctx"), 2)


def half_columns(half):
    return pl.ds(pl.multiple_of(half * HALF, HALF), HALF)


def params(limit=VMEM_LIMIT):
    return pltpu.CompilerParams(vmem_limit_bytes=limit)


def cost(flops, bytes_accessed):
    return pl.CostEstimate(flops=flops, bytes_accessed=bytes_accessed, transcendentals=0)


def coarse_kernel(k_ref, v_ref, q_ref, held_k, held_v, held_q, third_ref, own_ref, diag_ref, send_ref, mine_ref, fourth, sems):
    sources = ((k_ref, held_k), (v_ref, held_v), (q_ref, held_q))
    copies = [pltpu.make_async_copy(ref, held, sems.at[i]) for i, (ref, held) in enumerate(sources)]
    for copy in copies:
        copy.start()
    means = first_means()
    for i, copy in enumerate(copies):
        copy.wait()
        held = sources[i][1]
        for g in range(GROUPS):
            x = dot(means, held[GROUP * g : GROUP * (g + 1), :]).astype(BF16)
            x = rounded_slab_means(rounded_slab_means(x))
            if i < 2:
                start = BLOCK * i + 32 * g
                third_ref[start : start + 32, :] = x
            start = 64 * i + 16 * g
            fourth[start : start + 16, :] = rounded_slab_means(x)
    half = my_half()
    mine, theirs = half_columns(half), half_columns(1 - half)
    own_ref[...] = fourth[0:128, mine]
    mine_ref[...] = fourth[128:192, mine]
    diag_ref[...] = fourth[0:128, theirs]
    send_ref[...] = fourth[:, theirs]


def coarse(k, v, q):
    return pl.pallas_call(
        coarse_kernel,
        in_specs=[pl.BlockSpec(memory_space=pl.ANY)] * 3,
        out_shape=[pltpu.VMEM((ROWS, WIDTH), BF16)] * 3
        + [pltpu.VMEM((2 * BLOCK, WIDTH), BF16)]
        + [pltpu.VMEM((BLOCK, HALF), BF16)] * 2
        + [pltpu.VMEM((192, HALF), BF16), pltpu.VMEM((64, HALF), BF16)],
        scratch_shapes=[pltpu.VMEM((192, WIDTH), BF16), pltpu.SemaphoreType.DMA((3,))],
        cost_estimate=cost(4 * 10**8, 3 * 2**20),
        compiler_params=params(),
        name="coarse",
    )(*[pltpu.with_memory_space_constraint(x, pltpu.HBM) for x in (k, v, q)])


def gather_means(out_ref, chunks):
    means = pair_means(BLOCK)
    for i, chunk in enumerate(chunks):
        x = dot(means, chunk).astype(BF16)
        out_ref[32 * i : 32 * (i + 1)] = x[:32]
        out_ref[BLOCK + 32 * i : BLOCK + 32 * (i + 1)] = x[32:]


def halve(ref):
    means = pair_means(BLOCK)
    return jnp.concatenate([dot(means, ref[BLOCK * i : BLOCK * (i + 1)]).astype(BF16) for i in range(2)], axis=0)


def fifth_kernel(*refs):
    out_ref, next_ref = refs[-2:]
    gather_means(out_ref, [ref[0:BLOCK] for ref in refs[:-2]])
    next_ref[...] = halve(out_ref)


def seventh_kernel(line_ref, far_ref, across_ref, diagonal_ref, out_ref, next_ref):
    gather_means(out_ref, [line_ref[...], halve(far_ref), across_ref[...], diagonal_ref[...]])
    next_ref[...] = halve(out_ref)


def blocks(kernel, name, *chunks):
    return pl.pallas_call(
        kernel,
        out_shape=[jax.ShapeDtypeStruct((2 * BLOCK, HALF), BF16), jax.ShapeDtypeStruct((BLOCK, HALF), BF16)],
        cost_estimate=cost(10**8, 2**18),
        compiler_params=params(),
        name=name,
    )(*chunks)


def next_fronts(front):
    out = [front]
    for i in range(4):
        out.append(dot(spread_means(i), out[-1]).astype(BF16))
    return out


def local_kernel(first, order_ref, q_ref, k_ref, v_ref, att_ref, lse_ref, q3_ref):
    lane = lax.broadcasted_iota(jnp.int32, (SLABS, 8, HEAD_DIM), 2)
    slab = lax.broadcasted_iota(jnp.int32, (SLABS, 8, HEAD_DIM), 0)
    groups = range(GROUPS)
    rows = [slice(GROUP * g, GROUP * (g + 1)) for g in groups]
    means = first_means()

    def one_head(h, carry):
        into = pl.ds(pl.multiple_of(h * HEAD_DIM, HEAD_DIM), HEAD_DIM)
        col = pl.ds(pl.multiple_of((h + first) * HEAD_DIM, HEAD_DIM), HEAD_DIM)
        q0, q1, q2, kv1, kv2 = [], [], [], [], []
        for g in groups:
            front = dot(order_ref[...], q_ref[rows[g], col])
            q0.append(front.astype(BF16))
            q1.append(slab_means(front).astype(BF16))
            q2.append(rounded_slab_means(q1[g]))
            both = jnp.concatenate([k_ref[rows[g], col], v_ref[rows[g], col]], axis=1)
            kv1.append(dot(means, both).astype(BF16))
            kv2.append(rounded_slab_means(kv1[g]))
        q3_ref[:, into] = rounded_slab_means(jnp.concatenate(q2, axis=0))
        second = []
        for pair in range(2):
            far = jnp.concatenate(kv2[2 - 2 * pair : 4 - 2 * pair], axis=0)
            front = jnp.concatenate(q2[2 * pair : 2 * pair + 2], axis=0)
            second.append(attend(front, far[:, :HEAD_DIM], far[:, HEAD_DIM:]))
        for g in groups:
            part0 = attend(q0[g], k_ref[rows[g], col], v_ref[rows[g], col])
            far = kv1[g ^ 1]
            part1 = attend(q1[g], far[:, :HEAD_DIM], far[:, HEAD_DIM:])
            half = slice(64 * (g % 2), 64 * (g % 2 + 1))
            part2 = [x[half] for x in second[g // 2]]
            top, numer, denom = join(
                [
                    (*part0, 0.0),
                    (*[spread(x, 2) for x in part1], 1.0),
                    (*[spread(x, 4) for x in part2], 2.0),
                ]
            )
            att_ref[rows[g], into] = numer / denom
            lse = (top + jnp.log2(denom)).reshape(SLABS, 8, HEAD_DIM)
            lse_ref[h, g] = jnp.sum(jnp.where(lane == slab, lse, 0.0), axis=0)
        return carry

    lax.fori_loop(0, 2, one_head, 0)


def local(first, q, k, v):
    return pl.pallas_call(
        functools.partial(local_kernel, first),
        out_shape=[
            jax.ShapeDtypeStruct((ROWS, HALF), F32),
            jax.ShapeDtypeStruct((2, GROUPS, 8, 128), F32),
            jax.ShapeDtypeStruct((BLOCK, HALF), BF16),
        ],
        cost_estimate=cost(3 * 10**9, 3 * 2**20),
        compiler_params=params(),
        name="local_levels",
    )(order_matrix(), q, k, v)


def slab_lanes(x, copies):
    count = x.shape[0] // 8
    lane = lax.broadcasted_iota(jnp.int32, (count, 8, HEAD_DIM), 2)
    slab = lax.broadcasted_iota(jnp.int32, (count, 8, HEAD_DIM), 0)
    return jnp.sum(jnp.where(lane // copies == slab, x.reshape(count, 8, HEAD_DIM), 0.0), axis=0)


def third_kernel(near_ref, q3a_ref, q3b_ref, att_ref, lse_ref):
    for h in range(HEADS):
        col = slice(HEAD_DIM * h, HEAD_DIM * (h + 1))
        q3 = (q3a_ref, q3b_ref)[h // 2][:, HEAD_DIM * (h % 2) : HEAD_DIM * (h % 2 + 1)]
        top, numer, denom = attend(q3, near_ref[0:128, col], near_ref[128:256, col])
        att_ref[:, col] = numer / denom
        lse_ref[h] = slab_lanes(top + jnp.log2(denom) + 3.0, 1)


def third(near, q3s):
    return pl.pallas_call(
        third_kernel,
        out_shape=[jax.ShapeDtypeStruct((BLOCK, WIDTH), F32), jax.ShapeDtypeStruct((HEADS, 8, 128), F32)],
        cost_estimate=cost(10**8, 2**19),
        compiler_params=params(),
        name="third_level",
    )(near, *q3s)


def joined(one, other, col):
    return [jnp.concatenate([one[rows, col], other[rows, col]], axis=0) for rows in (slice(0, 64), slice(64, 128))]


def far_kernel(mine_ref, near_ref, *refs):
    fars, (att_ref, lse_ref, late_ref) = refs[:-3], refs[-3:]
    fronts = next_fronts(jnp.concatenate([mine_ref[...], near_ref[128:192]], axis=1))
    fronts = [jnp.concatenate([x[:, :HALF], x[:, HALF:]], axis=0) for x in fronts]
    late_ref[0:128] = fronts[3]
    late_ref[128:256] = fronts[4]
    across, diagonal, fifth_ref, across6, diagonal6 = fars
    for h in range(2):
        col = slice(HEAD_DIM * h, HEAD_DIM * (h + 1))
        pairs = [
            joined(across, diagonal, col),
            [fifth_ref[0:128, col], fifth_ref[128:256, col]],
            joined(across6, diagonal6, col),
        ]
        parts = [(*attend(fronts[i][:, col], *pair), 4.0 + i) for i, pair in enumerate(pairs)]
        top, numer, denom = join(parts)
        att_ref[:, col] = numer / denom
        lse_ref[:, col] = top + jnp.log2(denom)


def far_levels(mine, near, fars):
    return pl.pallas_call(
        far_kernel,
        out_shape=[
            jax.ShapeDtypeStruct((BLOCK, HALF), F32),
            jax.ShapeDtypeStruct((BLOCK, HALF), F32),
            jax.ShapeDtypeStruct((2 * BLOCK, HALF), BF16),
        ],
        cost_estimate=cost(5 * 10**8, 2**20),
        compiler_params=params(),
        name="far_levels",
    )(mine, near, *fars)


def last_kernel(late_ref, near_ref, across_ref, diagonal_ref, att_ref, lse_ref, own_ref, send_ref):
    for h in range(2):
        col = slice(HEAD_DIM * h, HEAD_DIM * (h + 1))
        got = attend(late_ref[0:128, col], near_ref[0:128, col], near_ref[128:256, col])
        far = joined(across_ref, diagonal_ref, col)
        parts = [(*got, 7.0), (*attend(late_ref[128:256, col], *far), 8.0)]
        top, numer, denom = join([(lse_ref[:, col], att_ref[:, col], 1.0, 0.0)] + parts)
        att = numer / denom
        peak = top + jnp.log2(denom)
        own_ref[0:64, col] = att[:64]
        own_ref[64:72, col] = slab_lanes(peak[:64], 2)
        send_ref[0:64, col] = att[64:].astype(BF16)
        peak = slab_lanes(peak[64:], 2)
        high = peak.astype(BF16).astype(F32)
        middle = (peak - high).astype(BF16).astype(F32)
        low = (peak - high - middle).astype(BF16).astype(F32)
        row = high + pltpu.roll(middle, 16, 1) + pltpu.roll(low, 32, 1)
        send_ref[64:80, col] = jnp.concatenate([row, row], axis=0).astype(BF16)


def last_level(*args):
    return pl.pallas_call(
        last_kernel,
        out_shape=[jax.ShapeDtypeStruct((72, HALF), F32), jax.ShapeDtypeStruct((80, HALF), BF16)],
        cost_estimate=cost(2 * 10**8, 2**19),
        compiler_params=params(),
        name="last_levels",
    )(*args)


def merge_kernel(own_ref, got_ref, att3_ref, lse3_ref, atta_ref, attb_ref, lsea_ref, lseb_ref, out_ref, ss_ref, far):
    half = my_half()
    far[:, half_columns(half)] = own_ref[...]
    theirs = half_columns(1 - half)
    far[0:64, theirs] = got_ref[0:64].astype(F32)
    row = got_ref[64:80].astype(F32)[:8]
    for h in range(2):
        part = row[:, HEAD_DIM * h : HEAD_DIM * (h + 1)]
        part = part + pltpu.roll(part, 112, 1) + pltpu.roll(part, 96, 1)
        far[64:72, pl.ds(pl.multiple_of((1 - half) * HALF + HEAD_DIM * h, HEAD_DIM), HEAD_DIM)] = part
    lane = lax.broadcasted_iota(jnp.int32, (8, 128), 1)
    means, shares = [], []
    for h in range(HEADS):
        col = slice(HEAD_DIM * h, HEAD_DIM * (h + 1))
        peak, old = far[64:72, col], lse3_ref[h]
        share = 1.0 / (1.0 + jnp.exp2(peak - old))
        rows = []
        for n in range(16):
            mean = far[8 * (n // 2) : 8 * (n // 2 + 1), col]
            rows.append(mean + share[:, n : n + 1] * (att3_ref[8 * n : 8 * (n + 1), col] - mean))
        means.append(rows)
        most = jnp.maximum(peak, old)
        peak = most + jnp.log2(jnp.exp2(peak - most) + jnp.exp2(old - most))
        row = []
        for g in range(GROUPS):
            other = jnp.zeros((8, 128), F32)
            for i in range(4):
                other = jnp.where(lane // 8 == i, peak[:, 4 * g + i : 4 * g + i + 1], other)
            row.append(1.0 / (1.0 + jnp.exp2(other - (lsea_ref, lseb_ref)[h // 2][h % 2, g])))
        shares.append(row)
    ones = jnp.ones((HEAD_DIM, HEAD_DIM), BF16)
    squares = jnp.zeros((8, 128), F32)
    for g in range(GROUPS):
        totals = []
        for i in range(SLABS):
            rows = slice(GROUP * g + 8 * i, GROUP * g + 8 * (i + 1))
            total = None
            for h in range(HEADS):
                near_ref = (atta_ref, attb_ref)[h // 2]
                near = near_ref[rows, HEAD_DIM * (h % 2) : HEAD_DIM * (h % 2 + 1)]
                mean = means[h][4 * g + i // 8]
                att = mean + shares[h][g][:, i : i + 1] * (near - mean)
                out_ref[rows, HEAD_DIM * h : HEAD_DIM * (h + 1)] = att
                total = att * att if total is None else total + att * att
            totals.append(total)
        total = jnp.concatenate(totals, axis=0)
        high = total.astype(BF16)
        low = (total - high.astype(F32)).astype(BF16)
        total = dot(high, ones) + dot(low, ones)
        for i in range(SLABS):
            squares = jnp.where(lane == g * SLABS + i, total[8 * i : 8 * (i + 1)], squares)
    ss_ref[...] = squares


def merge(*args):
    return pl.pallas_call(
        merge_kernel,
        out_shape=[jax.ShapeDtypeStruct((ROWS, WIDTH), F32), jax.ShapeDtypeStruct((8, 128), F32)],
        scratch_shapes=[pltpu.VMEM((72, WIDTH), F32)],
        cost_estimate=cost(10**8, 4 * 2**20),
        compiler_params=params(),
        name="merge",
    )(*args)


def finish_kernel(back_ref, ss_ref, gain_ref, att_ref, out_ref, held, sems):
    factor = lax.rsqrt(ss_ref[...] / FEAT + 1e-06)
    copies = []
    for g in range(GROUPS):
        pieces = []
        for i in range(SLABS):
            n = g * SLABS + i
            pieces.append(att_ref[8 * n : 8 * (n + 1), :] * factor[:, n : n + 1] * gain_ref[...])
        normed = jnp.concatenate(pieces, axis=0).astype(BF16)
        held[g] = dot(back_ref[...], normed).astype(BF16)
        copy = pltpu.make_async_copy(held.at[g], out_ref.at[pl.ds(GROUP * g, GROUP)], sems.at[g])
        copy.start()
        copies.append(copy)
    for copy in copies:
        copy.wait()


def finish(total, gain, att):
    return pl.pallas_call(
        finish_kernel,
        out_specs=pl.BlockSpec(memory_space=pl.ANY),
        out_shape=jax.ShapeDtypeStruct((ROWS, WIDTH), BF16),
        scratch_shapes=[pltpu.VMEM((GROUPS, GROUP, WIDTH), BF16), pltpu.SemaphoreType.DMA((GROUPS,))],
        cost_estimate=pl.CostEstimate(flops=3 * 10**8, bytes_accessed=3 * 2**20, transcendentals=0),
        compiler_params=pltpu.CompilerParams(vmem_limit_bytes=VMEM_LIMIT),
        name="finish",
    )(order_matrix().T, total, gain.reshape(1, WIDTH), att)


def after(args, *others):
    return lax.optimization_barrier((args, others))[0]


def body(queries, keys, values, norm_gain):
    count = lax.axis_size("ctx")

    def swap(x, mask):
        return lax.ppermute(x, "ctx", [(i, i ^ mask) for i in range(count)])

    def beside(first, sent, arrived):
        got = local(first, *after((held_q, held_k, held_v), *sent))
        return lax.optimization_barrier((got, arrived))

    held_k, held_v, held_q, own3, own, diag, send, mine = coarse(keys, values, queries)
    near4 = swap(send, 1)
    across = swap(own, 2)
    diagonal = swap(diag, 3)
    got, (near4, across, diagonal) = beside(0, (own, send), (near4, across, diagonal))
    locals_ = [got]
    own, line6 = blocks(fifth_kernel, "fifth_block", own, near4, across, diagonal)
    far5 = swap(own, 6)
    across6 = swap(line6, 8)
    diagonal6 = swap(line6, 14)
    got, (across6, diagonal6) = beside(2, (own, line6), (across6, diagonal6))
    locals_.append(got)
    last5 = own
    own, last = blocks(seventh_kernel, "seventh_block", line6, far5, across6, diagonal6)
    near7 = swap(own, 16)
    across8 = swap(last, 32)
    diagonal8 = swap(last, 48)
    near3 = swap(after(own3, last5), 1)
    mine = after(mine, last)
    att6, lse6, late = far_levels(mine, near4, [across, diagonal, far5, across6, diagonal6])
    kept, sent = last_level(late, near7, across8, diagonal8, att6, lse6)
    got = swap(sent, 1)
    att3, lse3 = third(near3, [x[2] for x in locals_])
    (atta, lsea), (attb, lseb) = [x[:2] for x in locals_]
    att, squares = merge(kept, got, att3, lse3, atta, attb, lsea, lseb)
    total = lax.psum(squares, "head")
    return finish(total, norm_gain, att)


def solution(mesh):
    return jax.shard_map(
        body,
        mesh=mesh,
        in_specs=(P("ctx", "head"), P("ctx", "head"), P("ctx", "head"), P("head")),
        out_specs=P("ctx", "head"),
        check_vma=False,
    )
```

```python
import functools
import math

import jax
import jax.numpy as jnp
import numpy as np
from jax import lax
from jax.experimental import pallas as pl
from jax.experimental.pallas import tpu as pltpu
from jax.sharding import PartitionSpec as P

HEAD_DIM = 128
BLOCK = 128
FEAT = 2048
HEADS = 4
ROWS = 1024
WIDTH = HEADS * HEAD_DIM
HALF = WIDTH // 2
GROUP = 256
GROUPS = ROWS // GROUP
SLABS = GROUP // 8
PORTIONS = ((0, 1), (2, 3))
SCALE = math.log2(math.e) / math.sqrt(HEAD_DIM)
BF16 = jnp.bfloat16
F32 = jnp.float32
VMEM_LIMIT = 48 * 1024 * 1024


def slab_order():
    token = np.arange(GROUP)
    return token // 128 * 128 + token % 16 * 8 + token // 16 % 8


def order_matrix():
    matrix = np.zeros((GROUP, GROUP), np.float32)
    matrix[slab_order(), np.arange(GROUP)] = 1.0
    return jnp.asarray(matrix, BF16)


def grid_of(rows, columns):
    row = lax.broadcasted_iota(jnp.int32, (rows, columns), 0)
    column = lax.broadcasted_iota(jnp.int32, (rows, columns), 1)
    return row, column


def halves(where):
    return jnp.where(where, 0.5, 0.0).astype(BF16)


def first_means():
    row, token = grid_of(GROUP // 2, GROUP)
    return halves(row == token // 128 * 64 + token % 16 // 2 * 8 + token // 16 % 8)


def pair_means(rows):
    row, column = grid_of(rows // 2, rows)
    return halves(column // 2 == row)


def spread_means(step):
    row, column = grid_of(64, 64)
    base = row // 2 ** (step + 1) * 2 ** (step + 1)
    return halves((column == base) | (column == base + 2**step))


def dot(a, b):
    return jnp.dot(a, b, preferred_element_type=F32)


def slab_means(x):
    rows, width = x.shape
    x = x.reshape(rows // 16, 2, 8, width)
    return ((x[:, 0] + x[:, 1]) * 0.5).reshape(rows // 2, width)


def rounded_slab_means(x):
    return slab_means(x.astype(F32)).astype(BF16)


def attend(front, keyset, valueset):
    scores = lax.dot_general(front, keyset, (((1,), (1,)), ((), ())), preferred_element_type=F32)
    top = jnp.max(scores, axis=-1, keepdims=True)
    weights = jnp.exp2((scores - top) * SCALE).astype(BF16)
    both = jnp.concatenate([valueset, jnp.ones(valueset.shape, BF16)], axis=1)
    sums = dot(weights, both)
    return jnp.broadcast_to(top * SCALE, (front.shape[0], HEAD_DIM)), sums[:, :HEAD_DIM], sums[:, HEAD_DIM:]


def join(parts):
    top = functools.reduce(jnp.maximum, [part[0] for part in parts])
    numer = denom = None
    for (peak, n, d), level in parts_with(parts):
        factor = jnp.exp2(peak - top + level)
        numer = n * factor if numer is None else numer + n * factor
        denom = d * factor if denom is None else denom + d * factor
    return top, numer, denom


def parts_with(parts):
    return [(part[:3], part[3]) for part in parts]


def spread(x, copies):
    rows, width = x.shape
    x = jnp.broadcast_to(x.reshape(rows // 8, 1, 8, width), (rows // 8, copies, 8, width))
    return x.reshape(rows * copies, width)


def my_half():
    return lax.rem(lax.axis_index("ctx"), 2)


def half_columns(half):
    return pl.ds(pl.multiple_of(half * HALF, HALF), HALF)


def params(limit=VMEM_LIMIT):
    return pltpu.CompilerParams(vmem_limit_bytes=limit)


def cost(flops, bytes_accessed):
    return pl.CostEstimate(flops=flops, bytes_accessed=bytes_accessed, transcendentals=0)


def coarse_kernel(k_ref, v_ref, q_ref, held_k, held_v, held_q, third_ref, own_ref, diag_ref, send_ref, mine_ref, fourth, sems):
    sources = ((k_ref, held_k), (v_ref, held_v), (q_ref, held_q))
    copies = [pltpu.make_async_copy(ref, held, sems.at[i]) for i, (ref, held) in enumerate(sources)]
    for copy in copies:
        copy.start()
    means = first_means()
    for i, copy in enumerate(copies):
        copy.wait()
        held = sources[i][1]
        for g in range(GROUPS):
            x = dot(means, held[GROUP * g : GROUP * (g + 1), :]).astype(BF16)
            x = rounded_slab_means(rounded_slab_means(x))
            if i < 2:
                start = BLOCK * i + 32 * g
                third_ref[start : start + 32, :] = x
            start = 64 * i + 16 * g
            fourth[start : start + 16, :] = rounded_slab_means(x)
    half = my_half()
    mine, theirs = half_columns(half), half_columns(1 - half)
    own_ref[...] = fourth[0:128, mine]
    mine_ref[...] = fourth[128:192, mine]
    diag_ref[...] = fourth[0:128, theirs]
    send_ref[...] = fourth[:, theirs]


def coarse(k, v, q):
    return pl.pallas_call(
        coarse_kernel,
        in_specs=[pl.BlockSpec(memory_space=pl.ANY)] * 3,
        out_shape=[pltpu.VMEM((ROWS, WIDTH), BF16)] * 3
        + [pltpu.VMEM((2 * BLOCK, WIDTH), BF16)]
        + [pltpu.VMEM((BLOCK, HALF), BF16)] * 2
        + [pltpu.VMEM((192, HALF), BF16), pltpu.VMEM((64, HALF), BF16)],
        scratch_shapes=[pltpu.VMEM((192, WIDTH), BF16), pltpu.SemaphoreType.DMA((3,))],
        cost_estimate=cost(4 * 10**8, 3 * 2**20),
        compiler_params=params(),
        name="coarse",
    )(*[pltpu.with_memory_space_constraint(x, pltpu.HBM) for x in (k, v, q)])


def gather_means(out_ref, chunks):
    means = pair_means(BLOCK)
    for i, chunk in enumerate(chunks):
        x = dot(means, chunk).astype(BF16)
        out_ref[32 * i : 32 * (i + 1)] = x[:32]
        out_ref[BLOCK + 32 * i : BLOCK + 32 * (i + 1)] = x[32:]


def halve(ref):
    means = pair_means(BLOCK)
    return jnp.concatenate([dot(means, ref[BLOCK * i : BLOCK * (i + 1)]).astype(BF16) for i in range(2)], axis=0)


def fifth_kernel(*refs):
    gather_means(refs[-1], [ref[0:BLOCK] for ref in refs[:-1]])


def halve_kernel(x_ref, out_ref):
    out_ref[...] = halve(x_ref)


def small(kernel, name, rows, *args):
    return pl.pallas_call(
        kernel,
        out_shape=jax.ShapeDtypeStruct((rows, HALF), BF16),
        cost_estimate=cost(10**8, 2**18),
        compiler_params=params(),
        name=name,
    )(*args)


def seventh_kernel(line_ref, far_ref, across_ref, diagonal_ref, out_ref, next_ref):
    gather_means(out_ref, [line_ref[...], halve(far_ref), across_ref[...], diagonal_ref[...]])
    next_ref[...] = halve(out_ref)


def blocks(kernel, name, *chunks):
    return pl.pallas_call(
        kernel,
        out_shape=[jax.ShapeDtypeStruct((2 * BLOCK, HALF), BF16), jax.ShapeDtypeStruct((BLOCK, HALF), BF16)],
        cost_estimate=cost(10**8, 2**18),
        compiler_params=params(),
        name=name,
    )(*chunks)


def next_fronts(front):
    out = [front]
    for i in range(4):
        out.append(dot(spread_means(i), out[-1]).astype(BF16))
    return out


def local_kernel(first, heads, order_ref, q_ref, k_ref, v_ref, att_ref, lse_ref, q3_ref):
    lane = lax.broadcasted_iota(jnp.int32, (SLABS, 8, HEAD_DIM), 2)
    slab = lax.broadcasted_iota(jnp.int32, (SLABS, 8, HEAD_DIM), 0)
    groups = range(GROUPS)
    rows = [slice(GROUP * g, GROUP * (g + 1)) for g in groups]
    means = first_means()

    def one_head(h, carry):
        into = pl.ds(pl.multiple_of(h * HEAD_DIM, HEAD_DIM), HEAD_DIM)
        col = pl.ds(pl.multiple_of((h + first) * HEAD_DIM, HEAD_DIM), HEAD_DIM)
        q0, q1, q2, kv1, kv2 = [], [], [], [], []
        for g in groups:
            front = dot(order_ref[...], q_ref[rows[g], col])
            q0.append(front.astype(BF16))
            q1.append(slab_means(front).astype(BF16))
            q2.append(rounded_slab_means(q1[g]))
            both = jnp.concatenate([k_ref[rows[g], col], v_ref[rows[g], col]], axis=1)
            kv1.append(dot(means, both).astype(BF16))
            kv2.append(rounded_slab_means(kv1[g]))
        q3_ref[:, into] = rounded_slab_means(jnp.concatenate(q2, axis=0))
        second = []
        for pair in range(2):
            far = jnp.concatenate(kv2[2 - 2 * pair : 4 - 2 * pair], axis=0)
            front = jnp.concatenate(q2[2 * pair : 2 * pair + 2], axis=0)
            second.append(attend(front, far[:, :HEAD_DIM], far[:, HEAD_DIM:]))
        for g in groups:
            part0 = attend(q0[g], k_ref[rows[g], col], v_ref[rows[g], col])
            far = kv1[g ^ 1]
            part1 = attend(q1[g], far[:, :HEAD_DIM], far[:, HEAD_DIM:])
            half = slice(64 * (g % 2), 64 * (g % 2 + 1))
            part2 = [x[half] for x in second[g // 2]]
            top, numer, denom = join(
                [
                    (*part0, 0.0),
                    (*[spread(x, 2) for x in part1], 1.0),
                    (*[spread(x, 4) for x in part2], 2.0),
                ]
            )
            att_ref[rows[g], into] = numer / denom
            lse = (top + jnp.log2(denom)).reshape(SLABS, 8, HEAD_DIM)
            lse_ref[h, g] = jnp.sum(jnp.where(lane == slab, lse, 0.0), axis=0)
        return carry

    lax.fori_loop(0, heads, one_head, 0)


def local(first, heads, q, k, v):
    return pl.pallas_call(
        functools.partial(local_kernel, first, heads),
        out_shape=[
            jax.ShapeDtypeStruct((ROWS, heads * HEAD_DIM), F32),
            jax.ShapeDtypeStruct((heads, GROUPS, 8, 128), F32),
            jax.ShapeDtypeStruct((BLOCK, heads * HEAD_DIM), BF16),
        ],
        cost_estimate=cost(3 * 10**9, 3 * 2**20),
        compiler_params=params(),
        name="local_levels",
    )(order_matrix(), q, k, v)


def slab_lanes(x, copies):
    count = x.shape[0] // 8
    lane = lax.broadcasted_iota(jnp.int32, (count, 8, HEAD_DIM), 2)
    slab = lax.broadcasted_iota(jnp.int32, (count, 8, HEAD_DIM), 0)
    return jnp.sum(jnp.where(lane // copies == slab, x.reshape(count, 8, HEAD_DIM), 0.0), axis=0)


def of_head(h, refs):
    for heads, ref in zip(PORTIONS, refs):
        if h in heads:
            return ref, heads.index(h)


def third_kernel(near_ref, *refs):
    q3_refs, (att_ref, lse_ref) = refs[:-2], refs[-2:]
    for h in range(HEADS):
        col = slice(HEAD_DIM * h, HEAD_DIM * (h + 1))
        ref, n = of_head(h, q3_refs)
        q3 = ref[:, HEAD_DIM * n : HEAD_DIM * (n + 1)]
        top, numer, denom = attend(q3, near_ref[0:128, col], near_ref[128:256, col])
        att_ref[:, col] = numer / denom
        lse_ref[h] = slab_lanes(top + jnp.log2(denom) + 3.0, 1)


def third(near, q3s):
    return pl.pallas_call(
        third_kernel,
        out_shape=[jax.ShapeDtypeStruct((BLOCK, WIDTH), F32), jax.ShapeDtypeStruct((HEADS, 8, 128), F32)],
        cost_estimate=cost(10**8, 2**19),
        compiler_params=params(),
        name="third_level",
    )(near, *q3s)


def joined(one, other, col):
    return [jnp.concatenate([one[rows, col], other[rows, col]], axis=0) for rows in (slice(0, 64), slice(64, 128))]


def fronts_kernel(mine_ref, near_ref, out_ref):
    fronts = next_fronts(jnp.concatenate([mine_ref[...], near_ref[128:192]], axis=1))
    for i, x in enumerate(fronts):
        out_ref[BLOCK * i : BLOCK * i + 64] = x[:, :HALF]
        out_ref[BLOCK * i + 64 : BLOCK * (i + 1)] = x[:, HALF:]


def far_kernel(fronts_ref, *refs):
    fars, (att_ref, lse_ref) = refs[:-2], refs[-2:]
    across, diagonal, fifth_ref, across6, diagonal6 = fars
    for h in range(2):
        col = slice(HEAD_DIM * h, HEAD_DIM * (h + 1))
        pairs = [
            joined(across, diagonal, col),
            [fifth_ref[0:128, col], fifth_ref[128:256, col]],
            joined(across6, diagonal6, col),
        ]
        parts = [
            (*attend(fronts_ref[BLOCK * i : BLOCK * (i + 1), col], *pair), 4.0 + i) for i, pair in enumerate(pairs)
        ]
        top, numer, denom = join(parts)
        att_ref[:, col] = numer / denom
        lse_ref[:, col] = top + jnp.log2(denom)


def far_levels(fronts, fars):
    return pl.pallas_call(
        far_kernel,
        out_shape=[
            jax.ShapeDtypeStruct((BLOCK, HALF), F32),
            jax.ShapeDtypeStruct((BLOCK, HALF), F32),
        ],
        cost_estimate=cost(5 * 10**8, 2**20),
        compiler_params=params(),
        name="far_levels",
    )(fronts, *fars)


def last_kernel(fronts_ref, near_ref, across_ref, diagonal_ref, att_ref, lse_ref, own_ref, send_ref):
    for h in range(2):
        col = slice(HEAD_DIM * h, HEAD_DIM * (h + 1))
        got = attend(fronts_ref[384:512, col], near_ref[0:128, col], near_ref[128:256, col])
        far = joined(across_ref, diagonal_ref, col)
        parts = [(*got, 7.0), (*attend(fronts_ref[512:640, col], *far), 8.0)]
        top, numer, denom = join([(lse_ref[:, col], att_ref[:, col], 1.0, 0.0)] + parts)
        att = numer / denom
        peak = top + jnp.log2(denom)
        own_ref[0:64, col] = att[:64]
        own_ref[64:72, col] = slab_lanes(peak[:64], 2)
        send_ref[0:64, col] = att[64:].astype(BF16)
        peak = slab_lanes(peak[64:], 2)
        high = peak.astype(BF16).astype(F32)
        middle = (peak - high).astype(BF16).astype(F32)
        low = (peak - high - middle).astype(BF16).astype(F32)
        row = high + pltpu.roll(middle, 16, 1) + pltpu.roll(low, 32, 1)
        send_ref[64:80, col] = jnp.concatenate([row, row], axis=0).astype(BF16)


def last_level(*args):
    return pl.pallas_call(
        last_kernel,
        out_shape=[jax.ShapeDtypeStruct((72, HALF), F32), jax.ShapeDtypeStruct((80, HALF), BF16)],
        cost_estimate=cost(2 * 10**8, 2**19),
        compiler_params=params(),
        name="last_levels",
    )(*args)


def merge_kernel(own_ref, got_ref, att3_ref, lse3_ref, *refs):
    out_ref, ss_ref, far = refs[-3:]
    count = len(PORTIONS)
    att_refs, lse_refs = refs[:count], refs[count : 2 * count]
    half = my_half()
    far[:, half_columns(half)] = own_ref[...]
    theirs = half_columns(1 - half)
    far[0:64, theirs] = got_ref[0:64].astype(F32)
    row = got_ref[64:80].astype(F32)[:8]
    for h in range(2):
        part = row[:, HEAD_DIM * h : HEAD_DIM * (h + 1)]
        part = part + pltpu.roll(part, 112, 1) + pltpu.roll(part, 96, 1)
        far[64:72, pl.ds(pl.multiple_of((1 - half) * HALF + HEAD_DIM * h, HEAD_DIM), HEAD_DIM)] = part
    lane = lax.broadcasted_iota(jnp.int32, (8, 128), 1)
    means, shares = [], []
    for h in range(HEADS):
        col = slice(HEAD_DIM * h, HEAD_DIM * (h + 1))
        peak, old = far[64:72, col], lse3_ref[h]
        share = 1.0 / (1.0 + jnp.exp2(peak - old))
        rows = []
        for n in range(16):
            mean = far[8 * (n // 2) : 8 * (n // 2 + 1), col]
            rows.append(mean + share[:, n : n + 1] * (att3_ref[8 * n : 8 * (n + 1), col] - mean))
        means.append(rows)
        most = jnp.maximum(peak, old)
        peak = most + jnp.log2(jnp.exp2(peak - most) + jnp.exp2(old - most))
        row = []
        for g in range(GROUPS):
            other = jnp.zeros((8, 128), F32)
            for i in range(4):
                other = jnp.where(lane // 8 == i, peak[:, 4 * g + i : 4 * g + i + 1], other)
            ref, n = of_head(h, lse_refs)
            row.append(1.0 / (1.0 + jnp.exp2(other - ref[n, g])))
        shares.append(row)
    ones = jnp.ones((HEAD_DIM, HEAD_DIM), BF16)
    squares = jnp.zeros((8, 128), F32)
    for g in range(GROUPS):
        totals = []
        for i in range(SLABS):
            rows = slice(GROUP * g + 8 * i, GROUP * g + 8 * (i + 1))
            total = None
            for h in range(HEADS):
                ref, n = of_head(h, att_refs)
                near = ref[rows, HEAD_DIM * n : HEAD_DIM * (n + 1)]
                mean = means[h][4 * g + i // 8]
                att = mean + shares[h][g][:, i : i + 1] * (near - mean)
                out_ref[rows, HEAD_DIM * h : HEAD_DIM * (h + 1)] = att
                total = att * att if total is None else total + att * att
            totals.append(total)
        total = jnp.concatenate(totals, axis=0)
        high = total.astype(BF16)
        low = (total - high.astype(F32)).astype(BF16)
        total = dot(high, ones) + dot(low, ones)
        for i in range(SLABS):
            squares = jnp.where(lane == g * SLABS + i, total[8 * i : 8 * (i + 1)], squares)
    ss_ref[...] = squares


def merge(*args):
    return pl.pallas_call(
        merge_kernel,
        out_shape=[jax.ShapeDtypeStruct((ROWS, WIDTH), F32), jax.ShapeDtypeStruct((8, 128), F32)],
        scratch_shapes=[pltpu.VMEM((72, WIDTH), F32)],
        cost_estimate=cost(10**8, 4 * 2**20),
        compiler_params=params(),
        name="merge",
    )(*args)


def finish_kernel(back_ref, ss_ref, gain_ref, att_ref, out_ref, held, sems):
    factor = lax.rsqrt(ss_ref[...] / FEAT + 1e-06)
    copies = []
    for g in range(GROUPS):
        pieces = []
        for i in range(SLABS):
            n = g * SLABS + i
            pieces.append(att_ref[8 * n : 8 * (n + 1), :] * factor[:, n : n + 1] * gain_ref[...])
        normed = jnp.concatenate(pieces, axis=0).astype(BF16)
        held[g] = dot(back_ref[...], normed).astype(BF16)
        copy = pltpu.make_async_copy(held.at[g], out_ref.at[pl.ds(GROUP * g, GROUP)], sems.at[g])
        copy.start()
        copies.append(copy)
    for copy in copies:
        copy.wait()


def finish(total, gain, att):
    return pl.pallas_call(
        finish_kernel,
        out_specs=pl.BlockSpec(memory_space=pl.ANY),
        out_shape=jax.ShapeDtypeStruct((ROWS, WIDTH), BF16),
        scratch_shapes=[pltpu.VMEM((GROUPS, GROUP, WIDTH), BF16), pltpu.SemaphoreType.DMA((GROUPS,))],
        cost_estimate=pl.CostEstimate(flops=3 * 10**8, bytes_accessed=3 * 2**20, transcendentals=0),
        compiler_params=pltpu.CompilerParams(vmem_limit_bytes=VMEM_LIMIT),
        name="finish",
    )(order_matrix().T, total, gain.reshape(1, WIDTH), att)


def after(args, *others):
    return lax.optimization_barrier((args, others))[0]


def body(queries, keys, values, norm_gain):
    count = lax.axis_size("ctx")

    def swap(x, mask):
        return lax.ppermute(x, "ctx", [(i, i ^ mask) for i in range(count)])

    def swap_heads(x, mask):
        return lax.ppermute(x, "head", [(i, i ^ mask) for i in range(lax.axis_size("head"))])

    def beside(portion, sent):
        heads = PORTIONS[portion]
        return local(heads[0], len(heads), *after((held_q, held_k, held_v), *sent))

    held_k, held_v, held_q, own3, own, diag, send, mine = coarse(keys, values, queries)
    near4 = swap(send, 1)
    across = swap(own, 2)
    diagonal = swap(diag, 3)
    got, (near4, across, diagonal) = lax.optimization_barrier((beside(0, (own, send)), (near4, across, diagonal)))
    locals_ = [got]
    own = small(fifth_kernel, "fifth_block", 2 * BLOCK, own, near4, across, diagonal)
    far5 = swap(own, 6)
    mine, near4 = after((mine, near4), own)
    fronts = small(fronts_kernel, "fronts", 5 * BLOCK, mine, near4)
    line6 = small(halve_kernel, "sixth_line", BLOCK, after(own, fronts))
    across6 = swap(line6, 8)
    diagonal6 = swap(line6, 14)
    near3 = swap(after(own3, line6), 1)
    got, (across6, diagonal6) = lax.optimization_barrier((beside(1, (line6,)), (across6, diagonal6)))
    locals_.append(got)
    own, last = blocks(seventh_kernel, "seventh_block", line6, far5, across6, diagonal6)
    near7 = swap(own, 16)
    across8 = swap(last, 32)
    diagonal8 = swap(last, 48)
    att6, lse6 = far_levels(after(fronts, last), [across, diagonal, far5, across6, diagonal6])
    kept, sent = last_level(fronts, near7, across8, diagonal8, att6, lse6)
    got = swap(sent, 1)
    att3, lse3 = third(near3, [x[2] for x in locals_])
    att, squares = merge(kept, got, att3, lse3, *[x[0] for x in locals_], *[x[1] for x in locals_])
    pair = swap_heads(squares, 1) + squares
    return finish(swap_heads(pair, 2) + pair, norm_gain, att)


def solution(mesh):
    return jax.shard_map(
        body,
        mesh=mesh,
        in_specs=(P("ctx", "head"), P("ctx", "head"), P("ctx", "head"), P("head")),
        out_specs=P("ctx", "head"),
        check_vma=False,
    )
```

```python
import functools
import math

import jax
import jax.numpy as jnp
import numpy as np
from jax import lax
from jax.experimental import pallas as pl
from jax.experimental.pallas import tpu as pltpu
from jax.sharding import PartitionSpec as P

HEAD_DIM = 128
BLOCK = 128
FEAT = 2048
HEADS = 4
ROWS = 1024
WIDTH = HEADS * HEAD_DIM
HALF = WIDTH // 2
GROUP = 256
GROUPS = ROWS // GROUP
SLABS = GROUP // 8
PORTIONS = ((0, 1), (2, 3))
SCALE = math.log2(math.e) / math.sqrt(HEAD_DIM)
BF16 = jnp.bfloat16
F32 = jnp.float32
VMEM_LIMIT = 48 * 1024 * 1024


def slab_order():
    token = np.arange(GROUP)
    return token // 128 * 128 + token % 16 * 8 + token // 16 % 8


def order_matrix():
    matrix = np.zeros((GROUP, GROUP), np.float32)
    matrix[slab_order(), np.arange(GROUP)] = 1.0
    return jnp.asarray(matrix, BF16)


def grid_of(rows, columns):
    row = lax.broadcasted_iota(jnp.int32, (rows, columns), 0)
    column = lax.broadcasted_iota(jnp.int32, (rows, columns), 1)
    return row, column


def halves(where):
    return jnp.where(where, 0.5, 0.0).astype(BF16)


def first_means():
    row, token = grid_of(GROUP // 2, GROUP)
    return halves(row == token // 128 * 64 + token % 16 // 2 * 8 + token // 16 % 8)


def pair_means(rows):
    row, column = grid_of(rows // 2, rows)
    return halves(column // 2 == row)


def spread_means(step):
    row, column = grid_of(64, 64)
    base = row // 2 ** (step + 1) * 2 ** (step + 1)
    return halves((column == base) | (column == base + 2**step))


def dot(a, b):
    return jnp.dot(a, b, preferred_element_type=F32)


def slab_means(x):
    rows, width = x.shape
    x = x.reshape(rows // 16, 2, 8, width)
    return ((x[:, 0] + x[:, 1]) * 0.5).reshape(rows // 2, width)


def rounded_slab_means(x):
    return slab_means(x.astype(F32)).astype(BF16)


def attend_all(triples):
    scores = [
        lax.dot_general(front, keyset, (((1,), (1,)), ((), ())), preferred_element_type=F32)
        for front, keyset, _ in triples
    ]
    tops = [jnp.max(s, axis=-1, keepdims=True) for s in scores]
    weights = [jnp.exp2((s - top) * SCALE).astype(BF16) for s, top in zip(scores, tops)]
    sums = [
        dot(w, jnp.concatenate([v, jnp.ones(v.shape, BF16)], axis=1)) for w, (_, _, v) in zip(weights, triples)
    ]
    return [
        (jnp.broadcast_to(top * SCALE, (top.shape[0], HEAD_DIM)), x[:, :HEAD_DIM], x[:, HEAD_DIM:])
        for top, x in zip(tops, sums)
    ]


def join(parts):
    top = functools.reduce(jnp.maximum, [part[0] for part in parts])
    numer = denom = None
    for (peak, n, d), level in parts_with(parts):
        factor = jnp.exp2(peak - top + level)
        numer = n * factor if numer is None else numer + n * factor
        denom = d * factor if denom is None else denom + d * factor
    return top, numer, denom


def parts_with(parts):
    return [(part[:3], part[3]) for part in parts]


def spread(x, copies):
    rows, width = x.shape
    x = jnp.broadcast_to(x.reshape(rows // 8, 1, 8, width), (rows // 8, copies, 8, width))
    return x.reshape(rows * copies, width)


def my_half():
    return lax.rem(lax.axis_index("ctx"), 2)


def half_columns(half):
    return pl.ds(pl.multiple_of(half * HALF, HALF), HALF)


def params(limit=VMEM_LIMIT):
    return pltpu.CompilerParams(vmem_limit_bytes=limit)


def cost(flops, bytes_accessed):
    return pl.CostEstimate(flops=flops, bytes_accessed=bytes_accessed, transcendentals=0)


def coarse_kernel(k_ref, v_ref, q_ref, held_k, held_v, held_q, third_ref, own_ref, diag_ref, send_ref, mine_ref, fourth, sems):
    sources = ((k_ref, held_k), (v_ref, held_v), (q_ref, held_q))
    copies = [pltpu.make_async_copy(ref, held, sems.at[i]) for i, (ref, held) in enumerate(sources)]
    for copy in copies:
        copy.start()
    means = first_means()
    for i, copy in enumerate(copies):
        copy.wait()
        held = sources[i][1]
        for g in range(GROUPS):
            x = dot(means, held[GROUP * g : GROUP * (g + 1), :]).astype(BF16)
            x = rounded_slab_means(rounded_slab_means(x))
            if i < 2:
                start = BLOCK * i + 32 * g
                third_ref[start : start + 32, :] = x
            start = 64 * i + 16 * g
            fourth[start : start + 16, :] = rounded_slab_means(x)
    half = my_half()
    mine, theirs = half_columns(half), half_columns(1 - half)
    own_ref[...] = fourth[0:128, mine]
    mine_ref[...] = fourth[128:192, mine]
    diag_ref[...] = fourth[0:128, theirs]
    send_ref[...] = fourth[:, theirs]


def coarse(k, v, q):
    return pl.pallas_call(
        coarse_kernel,
        in_specs=[pl.BlockSpec(memory_space=pl.ANY)] * 3,
        out_shape=[pltpu.VMEM((ROWS, WIDTH), BF16)] * 3
        + [pltpu.VMEM((2 * BLOCK, WIDTH), BF16)]
        + [pltpu.VMEM((BLOCK, HALF), BF16)] * 2
        + [pltpu.VMEM((192, HALF), BF16), pltpu.VMEM((64, HALF), BF16)],
        scratch_shapes=[pltpu.VMEM((192, WIDTH), BF16), pltpu.SemaphoreType.DMA((3,))],
        cost_estimate=cost(4 * 10**8, 3 * 2**20),
        compiler_params=params(),
        name="coarse",
    )(*[pltpu.with_memory_space_constraint(x, pltpu.HBM) for x in (k, v, q)])


def gather_means(out_ref, chunks):
    means = pair_means(BLOCK)
    for i, chunk in enumerate(chunks):
        x = dot(means, chunk).astype(BF16)
        out_ref[32 * i : 32 * (i + 1)] = x[:32]
        out_ref[BLOCK + 32 * i : BLOCK + 32 * (i + 1)] = x[32:]


def halve(ref):
    means = pair_means(BLOCK)
    return jnp.concatenate([dot(means, ref[BLOCK * i : BLOCK * (i + 1)]).astype(BF16) for i in range(2)], axis=0)


def fifth_kernel(*refs):
    gather_means(refs[-1], [ref[0:BLOCK] for ref in refs[:-1]])


def halve_kernel(x_ref, out_ref):
    out_ref[...] = halve(x_ref)


def small(kernel, name, rows, *args):
    return pl.pallas_call(
        kernel,
        out_shape=jax.ShapeDtypeStruct((rows, HALF), BF16),
        cost_estimate=cost(10**8, 2**18),
        compiler_params=params(),
        name=name,
    )(*args)


def seventh_kernel(line_ref, far_ref, across_ref, diagonal_ref, out_ref, next_ref):
    gather_means(out_ref, [line_ref[...], halve(far_ref), across_ref[...], diagonal_ref[...]])
    next_ref[...] = halve(out_ref)


def blocks(kernel, name, *chunks):
    return pl.pallas_call(
        kernel,
        out_shape=[jax.ShapeDtypeStruct((2 * BLOCK, HALF), BF16), jax.ShapeDtypeStruct((BLOCK, HALF), BF16)],
        cost_estimate=cost(10**8, 2**18),
        compiler_params=params(),
        name=name,
    )(*chunks)


def next_fronts(front):
    out = [front]
    for i in range(4):
        out.append(dot(spread_means(i), out[-1]).astype(BF16))
    return out


def local_kernel(first, heads, order_ref, q_ref, k_ref, v_ref, att_ref, lse_ref, q3_ref):
    lane = lax.broadcasted_iota(jnp.int32, (SLABS, 8, HEAD_DIM), 2)
    slab = lax.broadcasted_iota(jnp.int32, (SLABS, 8, HEAD_DIM), 0)
    groups = range(GROUPS)
    rows = [slice(GROUP * g, GROUP * (g + 1)) for g in groups]
    means = first_means()

    def one_head(h, carry):
        into = pl.ds(pl.multiple_of(h * HEAD_DIM, HEAD_DIM), HEAD_DIM)
        col = pl.ds(pl.multiple_of((h + first) * HEAD_DIM, HEAD_DIM), HEAD_DIM)
        q0, q1, q2, kv1, kv2 = [], [], [], [], []
        for g in groups:
            front = dot(order_ref[...], q_ref[rows[g], col])
            q0.append(front.astype(BF16))
            q1.append(slab_means(front).astype(BF16))
            q2.append(rounded_slab_means(q1[g]))
            both = jnp.concatenate([k_ref[rows[g], col], v_ref[rows[g], col]], axis=1)
            kv1.append(dot(means, both).astype(BF16))
            kv2.append(rounded_slab_means(kv1[g]))
        q3_ref[:, into] = rounded_slab_means(jnp.concatenate(q2, axis=0))
        far = [jnp.concatenate(kv2[2 - 2 * pair : 4 - 2 * pair], axis=0) for pair in range(2)]
        front = [jnp.concatenate(q2[2 * pair : 2 * pair + 2], axis=0) for pair in range(2)]
        triples = [(q, kv[:, :HEAD_DIM], kv[:, HEAD_DIM:]) for q, kv in zip(front, far)]
        for g in groups:
            far = kv1[g ^ 1]
            triples.append((q0[g], k_ref[rows[g], col], v_ref[rows[g], col]))
            triples.append((q1[g], far[:, :HEAD_DIM], far[:, HEAD_DIM:]))
        second = attend_all(triples)
        for g in groups:
            part0, part1 = second[2 * g + 2 : 2 * g + 4]
            half = slice(64 * (g % 2), 64 * (g % 2 + 1))
            part2 = [x[half] for x in second[g // 2]]
            top, numer, denom = join(
                [
                    (*part0, 0.0),
                    (*[spread(x, 2) for x in part1], 1.0),
                    (*[spread(x, 4) for x in part2], 2.0),
                ]
            )
            att_ref[rows[g], into] = numer / denom
            lse = (top + jnp.log2(denom)).reshape(SLABS, 8, HEAD_DIM)
            lse_ref[h, g] = jnp.sum(jnp.where(lane == slab, lse, 0.0), axis=0)
        return carry

    lax.fori_loop(0, heads, one_head, 0, unroll=True)


def local(first, heads, q, k, v):
    return pl.pallas_call(
        functools.partial(local_kernel, first, heads),
        out_shape=[
            jax.ShapeDtypeStruct((ROWS, heads * HEAD_DIM), F32),
            jax.ShapeDtypeStruct((heads, GROUPS, 8, 128), F32),
            jax.ShapeDtypeStruct((BLOCK, heads * HEAD_DIM), BF16),
        ],
        cost_estimate=cost(3 * 10**9, 3 * 2**20),
        compiler_params=params(),
        name="local_levels",
    )(order_matrix(), q, k, v)


def slab_lanes(x, copies):
    count = x.shape[0] // 8
    lane = lax.broadcasted_iota(jnp.int32, (count, 8, HEAD_DIM), 2)
    slab = lax.broadcasted_iota(jnp.int32, (count, 8, HEAD_DIM), 0)
    return jnp.sum(jnp.where(lane // copies == slab, x.reshape(count, 8, HEAD_DIM), 0.0), axis=0)


def of_head(h, refs):
    for heads, ref in zip(PORTIONS, refs):
        if h in heads:
            return ref, heads.index(h)


def third_kernel(near_ref, *refs):
    q3_refs, (att_ref, lse_ref) = refs[:-2], refs[-2:]
    cols = [slice(HEAD_DIM * h, HEAD_DIM * (h + 1)) for h in range(HEADS)]
    triples = []
    for h, col in enumerate(cols):
        ref, n = of_head(h, q3_refs)
        triples.append((ref[:, HEAD_DIM * n : HEAD_DIM * (n + 1)], near_ref[0:128, col], near_ref[128:256, col]))
    for h, (top, numer, denom) in enumerate(attend_all(triples)):
        att_ref[:, cols[h]] = numer / denom
        lse_ref[h] = slab_lanes(top + jnp.log2(denom) + 3.0, 1)


def third(near, q3s):
    return pl.pallas_call(
        third_kernel,
        out_shape=[jax.ShapeDtypeStruct((BLOCK, WIDTH), F32), jax.ShapeDtypeStruct((HEADS, 8, 128), F32)],
        cost_estimate=cost(10**8, 2**19),
        compiler_params=params(),
        name="third_level",
    )(near, *q3s)


def joined(one, other, col):
    return [jnp.concatenate([one[rows, col], other[rows, col]], axis=0) for rows in (slice(0, 64), slice(64, 128))]


def fronts_kernel(mine_ref, near_ref, out_ref):
    fronts = next_fronts(jnp.concatenate([mine_ref[...], near_ref[128:192]], axis=1))
    for i, x in enumerate(fronts):
        out_ref[BLOCK * i : BLOCK * i + 64] = x[:, :HALF]
        out_ref[BLOCK * i + 64 : BLOCK * (i + 1)] = x[:, HALF:]


def far_kernel(fronts_ref, *refs):
    fars, (att_ref, lse_ref) = refs[:-2], refs[-2:]
    across, diagonal, fifth_ref, across6, diagonal6 = fars
    cols = [slice(HEAD_DIM * h, HEAD_DIM * (h + 1)) for h in range(2)]
    triples = []
    for col in cols:
        pairs = [
            joined(across, diagonal, col),
            [fifth_ref[0:128, col], fifth_ref[128:256, col]],
            joined(across6, diagonal6, col),
        ]
        triples += [(fronts_ref[BLOCK * i : BLOCK * (i + 1), col], *pair) for i, pair in enumerate(pairs)]
    got = attend_all(triples)
    for h, col in enumerate(cols):
        parts = [(*got[3 * h + i], 4.0 + i) for i in range(3)]
        top, numer, denom = join(parts)
        att_ref[:, col] = numer / denom
        lse_ref[:, col] = top + jnp.log2(denom)


def far_levels(fronts, fars):
    return pl.pallas_call(
        far_kernel,
        out_shape=[
            jax.ShapeDtypeStruct((BLOCK, HALF), F32),
            jax.ShapeDtypeStruct((BLOCK, HALF), F32),
        ],
        cost_estimate=cost(5 * 10**8, 2**20),
        compiler_params=params(),
        name="far_levels",
    )(fronts, *fars)


def last_kernel(fronts_ref, near_ref, across_ref, diagonal_ref, att_ref, lse_ref, own_ref, send_ref):
    cols = [slice(HEAD_DIM * h, HEAD_DIM * (h + 1)) for h in range(2)]
    triples = []
    for col in cols:
        triples.append((fronts_ref[384:512, col], near_ref[0:128, col], near_ref[128:256, col]))
        triples.append((fronts_ref[512:640, col], *joined(across_ref, diagonal_ref, col)))
    got = attend_all(triples)
    for h, col in enumerate(cols):
        parts = [(*got[2 * h], 7.0), (*got[2 * h + 1], 8.0)]
        top, numer, denom = join([(lse_ref[:, col], att_ref[:, col], 1.0, 0.0)] + parts)
        att = numer / denom
        peak = top + jnp.log2(denom)
        own_ref[0:64, col] = att[:64]
        own_ref[64:72, col] = slab_lanes(peak[:64], 2)
        send_ref[0:64, col] = att[64:].astype(BF16)
        peak = slab_lanes(peak[64:], 2)
        high = peak.astype(BF16).astype(F32)
        middle = (peak - high).astype(BF16).astype(F32)
        low = (peak - high - middle).astype(BF16).astype(F32)
        row = high + pltpu.roll(middle, 16, 1) + pltpu.roll(low, 32, 1)
        send_ref[64:80, col] = jnp.concatenate([row, row], axis=0).astype(BF16)


def last_level(*args):
    return pl.pallas_call(
        last_kernel,
        out_shape=[jax.ShapeDtypeStruct((72, HALF), F32), jax.ShapeDtypeStruct((80, HALF), BF16)],
        cost_estimate=cost(2 * 10**8, 2**19),
        compiler_params=params(),
        name="last_levels",
    )(*args)


def merge_kernel(own_ref, got_ref, att3_ref, lse3_ref, *refs):
    out_ref, ss_ref, far = refs[-3:]
    count = len(PORTIONS)
    att_refs, lse_refs = refs[:count], refs[count : 2 * count]
    half = my_half()
    far[:, half_columns(half)] = own_ref[...]
    theirs = half_columns(1 - half)
    far[0:64, theirs] = got_ref[0:64].astype(F32)
    row = got_ref[64:80].astype(F32)[:8]
    for h in range(2):
        part = row[:, HEAD_DIM * h : HEAD_DIM * (h + 1)]
        part = part + pltpu.roll(part, 112, 1) + pltpu.roll(part, 96, 1)
        far[64:72, pl.ds(pl.multiple_of((1 - half) * HALF + HEAD_DIM * h, HEAD_DIM), HEAD_DIM)] = part
    lane = lax.broadcasted_iota(jnp.int32, (8, 128), 1)
    means, shares = [], []
    for h in range(HEADS):
        col = slice(HEAD_DIM * h, HEAD_DIM * (h + 1))
        peak, old = far[64:72, col], lse3_ref[h]
        share = 1.0 / (1.0 + jnp.exp2(peak - old))
        rows = []
        for n in range(16):
            mean = far[8 * (n // 2) : 8 * (n // 2 + 1), col]
            rows.append(mean + share[:, n : n + 1] * (att3_ref[8 * n : 8 * (n + 1), col] - mean))
        means.append(rows)
        most = jnp.maximum(peak, old)
        peak = most + jnp.log2(jnp.exp2(peak - most) + jnp.exp2(old - most))
        row = []
        for g in range(GROUPS):
            other = jnp.zeros((8, 128), F32)
            for i in range(4):
                other = jnp.where(lane // 8 == i, peak[:, 4 * g + i : 4 * g + i + 1], other)
            ref, n = of_head(h, lse_refs)
            row.append(1.0 / (1.0 + jnp.exp2(other - ref[n, g])))
        shares.append(row)
    ones = jnp.ones((HEAD_DIM, HEAD_DIM), BF16)
    squares = jnp.zeros((8, 128), F32)
    for g in range(GROUPS):
        totals = []
        for i in range(SLABS):
            rows = slice(GROUP * g + 8 * i, GROUP * g + 8 * (i + 1))
            total = None
            for h in range(HEADS):
                ref, n = of_head(h, att_refs)
                near = ref[rows, HEAD_DIM * n : HEAD_DIM * (n + 1)]
                mean = means[h][4 * g + i // 8]
                att = mean + shares[h][g][:, i : i + 1] * (near - mean)
                out_ref[rows, HEAD_DIM * h : HEAD_DIM * (h + 1)] = att
                total = att * att if total is None else total + att * att
            totals.append(total)
        total = jnp.concatenate(totals, axis=0)
        high = total.astype(BF16)
        low = (total - high.astype(F32)).astype(BF16)
        total = dot(high, ones) + dot(low, ones)
        for i in range(SLABS):
            squares = jnp.where(lane == g * SLABS + i, total[8 * i : 8 * (i + 1)], squares)
    ss_ref[...] = squares


def merge(*args):
    return pl.pallas_call(
        merge_kernel,
        out_shape=[jax.ShapeDtypeStruct((ROWS, WIDTH), F32), jax.ShapeDtypeStruct((8, 128), F32)],
        scratch_shapes=[pltpu.VMEM((72, WIDTH), F32)],
        cost_estimate=cost(10**8, 4 * 2**20),
        compiler_params=params(),
        name="merge",
    )(*args)


def finish_kernel(back_ref, ss_ref, gain_ref, att_ref, out_ref, held, sems):
    factor = lax.rsqrt(ss_ref[...] / FEAT + 1e-06)
    copies = []
    for g in range(GROUPS):
        pieces = []
        for i in range(SLABS):
            n = g * SLABS + i
            pieces.append(att_ref[8 * n : 8 * (n + 1), :] * factor[:, n : n + 1] * gain_ref[...])
        normed = jnp.concatenate(pieces, axis=0).astype(BF16)
        held[g] = dot(back_ref[...], normed).astype(BF16)
        copy = pltpu.make_async_copy(held.at[g], out_ref.at[pl.ds(GROUP * g, GROUP)], sems.at[g])
        copy.start()
        copies.append(copy)
    for copy in copies:
        copy.wait()


def finish(total, gain, att):
    return pl.pallas_call(
        finish_kernel,
        out_specs=pl.BlockSpec(memory_space=pl.ANY),
        out_shape=jax.ShapeDtypeStruct((ROWS, WIDTH), BF16),
        scratch_shapes=[pltpu.VMEM((GROUPS, GROUP, WIDTH), BF16), pltpu.SemaphoreType.DMA((GROUPS,))],
        cost_estimate=pl.CostEstimate(flops=3 * 10**8, bytes_accessed=3 * 2**20, transcendentals=0),
        compiler_params=pltpu.CompilerParams(vmem_limit_bytes=VMEM_LIMIT),
        name="finish",
    )(order_matrix().T, total, gain.reshape(1, WIDTH), att)


def after(args, *others):
    return lax.optimization_barrier((args, others))[0]


def body(queries, keys, values, norm_gain):
    count = lax.axis_size("ctx")

    def swap(x, mask):
        return lax.ppermute(x, "ctx", [(i, i ^ mask) for i in range(count)])

    def swap_heads(x, mask):
        return lax.ppermute(x, "head", [(i, i ^ mask) for i in range(lax.axis_size("head"))])

    def beside(portion, sent):
        heads = PORTIONS[portion]
        return local(heads[0], len(heads), *after((held_q, held_k, held_v), *sent))

    held_k, held_v, held_q, own3, own, diag, send, mine = coarse(keys, values, queries)
    near4 = swap(send, 1)
    across = swap(own, 2)
    diagonal = swap(diag, 3)
    got, (near4, across, diagonal) = lax.optimization_barrier((beside(0, (own, send)), (near4, across, diagonal)))
    locals_ = [got]
    own = small(fifth_kernel, "fifth_block", 2 * BLOCK, own, near4, across, diagonal)
    far5 = swap(own, 6)
    mine, near4 = after((mine, near4), own)
    fronts = small(fronts_kernel, "fronts", 5 * BLOCK, mine, near4)
    line6 = small(halve_kernel, "sixth_line", BLOCK, after(own, fronts))
    across6 = swap(line6, 8)
    diagonal6 = swap(line6, 14)
    near3 = swap(after(own3, line6), 1)
    got, (across6, diagonal6) = lax.optimization_barrier((beside(1, (line6,)), (across6, diagonal6)))
    locals_.append(got)
    own, last = blocks(seventh_kernel, "seventh_block", line6, far5, across6, diagonal6)
    near7 = swap(own, 16)
    across8 = swap(last, 32)
    diagonal8 = swap(last, 48)
    att6, lse6 = far_levels(after(fronts, last), [across, diagonal, far5, across6, diagonal6])
    kept, sent = last_level(fronts, near7, across8, diagonal8, att6, lse6)
    got = swap(sent, 1)
    att3, lse3 = third(near3, [x[2] for x in locals_])
    att, squares = merge(kept, got, att3, lse3, *[x[0] for x in locals_], *[x[1] for x in locals_])
    pair = swap_heads(squares, 1) + squares
    return finish(swap_heads(pair, 2) + pair, norm_gain, att)


def solution(mesh):
    return jax.shard_map(
        body,
        mesh=mesh,
        in_specs=(P("ctx", "head"), P("ctx", "head"), P("ctx", "head"), P("head")),
        out_specs=P("ctx", "head"),
        check_vma=False,
    )
```

```python
import functools
import math

import jax
import jax.numpy as jnp
import numpy as np
from jax import lax
from jax.experimental import pallas as pl
from jax.experimental.pallas import tpu as pltpu
from jax.sharding import PartitionSpec as P

HEAD_DIM = 128
BLOCK = 128
FEAT = 2048
HEADS = 4
ROWS = 1024
WIDTH = HEADS * HEAD_DIM
HALF = WIDTH // 2
GROUP = 256
GROUPS = ROWS // GROUP
SLABS = GROUP // 8
PORTIONS = ((0, 1), (2, 3))
SCALE = math.log2(math.e) / math.sqrt(HEAD_DIM)
BF16 = jnp.bfloat16
F32 = jnp.float32
VMEM_LIMIT = 48 * 1024 * 1024


def slab_order():
    token = np.arange(GROUP)
    return token // 128 * 128 + token % 16 * 8 + token // 16 % 8


def order_matrix():
    matrix = np.zeros((GROUP, GROUP), np.float32)
    matrix[slab_order(), np.arange(GROUP)] = 1.0
    return jnp.asarray(matrix, BF16)


def grid_of(rows, columns):
    row = lax.broadcasted_iota(jnp.int32, (rows, columns), 0)
    column = lax.broadcasted_iota(jnp.int32, (rows, columns), 1)
    return row, column


def halves(where):
    return jnp.where(where, 0.5, 0.0).astype(BF16)


def first_means():
    row, token = grid_of(GROUP // 2, GROUP)
    return halves(row == token // 128 * 64 + token % 16 // 2 * 8 + token // 16 % 8)


def pair_means(rows):
    row, column = grid_of(rows // 2, rows)
    return halves(column // 2 == row)


def spread_means(step):
    row, column = grid_of(64, 64)
    base = row // 2 ** (step + 1) * 2 ** (step + 1)
    return halves((column == base) | (column == base + 2**step))


def dot(a, b):
    return jnp.dot(a, b, preferred_element_type=F32)


def slab_means(x):
    rows, width = x.shape
    x = x.reshape(rows // 16, 2, 8, width)
    return ((x[:, 0] + x[:, 1]) * 0.5).reshape(rows // 2, width)


def rounded_slab_means(x):
    return slab_means(x.astype(F32)).astype(BF16)


def attend_all(triples):
    scores = [
        lax.dot_general(front, keyset, (((1,), (1,)), ((), ())), preferred_element_type=F32)
        for front, keyset, _ in triples
    ]
    tops = [jnp.max(s, axis=-1, keepdims=True) for s in scores]
    weights = [jnp.exp2((s - top) * SCALE).astype(BF16) for s, top in zip(scores, tops)]
    sums = [
        dot(w, jnp.concatenate([v, jnp.ones(v.shape, BF16)], axis=1)) for w, (_, _, v) in zip(weights, triples)
    ]
    return [
        (jnp.broadcast_to(top * SCALE, (top.shape[0], HEAD_DIM)), x[:, :HEAD_DIM], x[:, HEAD_DIM:])
        for top, x in zip(tops, sums)
    ]


def join(parts):
    top = functools.reduce(jnp.maximum, [part[0] for part in parts])
    numer = denom = None
    for (peak, n, d), level in parts_with(parts):
        factor = jnp.exp2(peak - top + level)
        numer = n * factor if numer is None else numer + n * factor
        denom = d * factor if denom is None else denom + d * factor
    return top, numer, denom


def parts_with(parts):
    return [(part[:3], part[3]) for part in parts]


def spread(x, copies):
    rows, width = x.shape
    x = jnp.broadcast_to(x.reshape(rows // 8, 1, 8, width), (rows // 8, copies, 8, width))
    return x.reshape(rows * copies, width)


def my_half():
    return lax.rem(lax.axis_index("ctx"), 2)


def half_columns(half):
    return pl.ds(pl.multiple_of(half * HALF, HALF), HALF)


def params(limit=VMEM_LIMIT):
    return pltpu.CompilerParams(vmem_limit_bytes=limit)


def cost(flops, bytes_accessed):
    return pl.CostEstimate(flops=flops, bytes_accessed=bytes_accessed, transcendentals=0)


def coarse_kernel(k_ref, v_ref, q_ref, held_k, held_v, held_q, third_ref, own_ref, diag_ref, send_ref, mine_ref, fourth, sems):
    sources = ((k_ref, held_k), (v_ref, held_v), (q_ref, held_q))
    copies = [pltpu.make_async_copy(ref, held, sems.at[i]) for i, (ref, held) in enumerate(sources)]
    for copy in copies:
        copy.start()
    means = first_means()
    for i, copy in enumerate(copies):
        copy.wait()
        held = sources[i][1]
        for g in range(GROUPS):
            x = dot(means, held[GROUP * g : GROUP * (g + 1), :]).astype(BF16)
            x = rounded_slab_means(rounded_slab_means(x))
            if i < 2:
                start = BLOCK * i + 32 * g
                third_ref[start : start + 32, :] = x
            start = 64 * i + 16 * g
            fourth[start : start + 16, :] = rounded_slab_means(x)
    half = my_half()
    mine, theirs = half_columns(half), half_columns(1 - half)
    own_ref[...] = fourth[0:128, mine]
    mine_ref[...] = fourth[128:192, mine]
    diag_ref[...] = fourth[0:128, theirs]
    send_ref[...] = fourth[:, theirs]


def coarse(k, v, q):
    return pl.pallas_call(
        coarse_kernel,
        in_specs=[pl.BlockSpec(memory_space=pl.ANY)] * 3,
        out_shape=[pltpu.VMEM((ROWS, WIDTH), BF16)] * 3
        + [pltpu.VMEM((2 * BLOCK, WIDTH), BF16)]
        + [pltpu.VMEM((BLOCK, HALF), BF16)] * 2
        + [pltpu.VMEM((192, HALF), BF16), pltpu.VMEM((64, HALF), BF16)],
        scratch_shapes=[pltpu.VMEM((192, WIDTH), BF16), pltpu.SemaphoreType.DMA((3,))],
        cost_estimate=cost(4 * 10**8, 3 * 2**20),
        compiler_params=params(),
        name="coarse",
    )(*[pltpu.with_memory_space_constraint(x, pltpu.HBM) for x in (k, v, q)])


def gather_means(out_ref, chunks):
    means = pair_means(BLOCK)
    for i, chunk in enumerate(chunks):
        x = dot(means, chunk).astype(BF16)
        out_ref[32 * i : 32 * (i + 1)] = x[:32]
        out_ref[BLOCK + 32 * i : BLOCK + 32 * (i + 1)] = x[32:]


def halve(ref):
    means = pair_means(BLOCK)
    return jnp.concatenate([dot(means, ref[BLOCK * i : BLOCK * (i + 1)]).astype(BF16) for i in range(2)], axis=0)


def fifth_kernel(*refs):
    gather_means(refs[-1], [ref[0:BLOCK] for ref in refs[:-1]])


def halve_kernel(x_ref, out_ref):
    out_ref[...] = halve(x_ref)


def small(kernel, name, rows, *args):
    return pl.pallas_call(
        kernel,
        out_shape=jax.ShapeDtypeStruct((rows, HALF), BF16),
        cost_estimate=cost(10**8, 2**18),
        compiler_params=params(),
        name=name,
    )(*args)


def seventh_kernel(line_ref, far_ref, across_ref, diagonal_ref, out_ref, next_ref):
    gather_means(out_ref, [line_ref[...], halve(far_ref), across_ref[...], diagonal_ref[...]])
    next_ref[...] = halve(out_ref)


def blocks(kernel, name, *chunks):
    return pl.pallas_call(
        kernel,
        out_shape=[jax.ShapeDtypeStruct((2 * BLOCK, HALF), BF16), jax.ShapeDtypeStruct((BLOCK, HALF), BF16)],
        cost_estimate=cost(10**8, 2**18),
        compiler_params=params(),
        name=name,
    )(*chunks)


def next_fronts(front):
    out = [front]
    for i in range(4):
        out.append(dot(spread_means(i), out[-1]).astype(BF16))
    return out


def local_kernel(first, heads, order_ref, q_ref, k_ref, v_ref, att_ref, lse_ref, q3_ref):
    lane = lax.broadcasted_iota(jnp.int32, (SLABS, 8, HEAD_DIM), 2)
    slab = lax.broadcasted_iota(jnp.int32, (SLABS, 8, HEAD_DIM), 0)
    groups = range(GROUPS)
    rows = [slice(GROUP * g, GROUP * (g + 1)) for g in groups]
    means = first_means()

    def one_head(h, carry):
        into = pl.ds(pl.multiple_of(h * HEAD_DIM, HEAD_DIM), HEAD_DIM)
        col = pl.ds(pl.multiple_of((h + first) * HEAD_DIM, HEAD_DIM), HEAD_DIM)
        q0, q1, q2, kv1, kv2 = [], [], [], [], []
        for g in groups:
            front = dot(order_ref[...], q_ref[rows[g], col])
            q0.append(front.astype(BF16))
            q1.append(slab_means(front).astype(BF16))
            q2.append(rounded_slab_means(q1[g]))
            both = jnp.concatenate([k_ref[rows[g], col], v_ref[rows[g], col]], axis=1)
            kv1.append(dot(means, both).astype(BF16))
            kv2.append(rounded_slab_means(kv1[g]))
        q3_ref[:, into] = rounded_slab_means(jnp.concatenate(q2, axis=0))
        far = [jnp.concatenate(kv2[2 - 2 * pair : 4 - 2 * pair], axis=0) for pair in range(2)]
        front = [jnp.concatenate(q2[2 * pair : 2 * pair + 2], axis=0) for pair in range(2)]
        triples = [(q, kv[:, :HEAD_DIM], kv[:, HEAD_DIM:]) for q, kv in zip(front, far)]
        for g in groups:
            far = kv1[g ^ 1]
            triples.append((q0[g], k_ref[rows[g], col], v_ref[rows[g], col]))
            triples.append((q1[g], far[:, :HEAD_DIM], far[:, HEAD_DIM:]))
        second = attend_all(triples)
        for g in groups:
            part0, part1 = second[2 * g + 2 : 2 * g + 4]
            half = slice(64 * (g % 2), 64 * (g % 2 + 1))
            part2 = [x[half] for x in second[g // 2]]
            top, numer, denom = join(
                [
                    (*part0, 0.0),
                    (*[spread(x, 2) for x in part1], 1.0),
                    (*[spread(x, 4) for x in part2], 2.0),
                ]
            )
            att_ref[rows[g], into] = numer / denom
            lse = (top + jnp.log2(denom)).reshape(SLABS, 8, HEAD_DIM)
            lse_ref[h, g] = jnp.sum(jnp.where(lane == slab, lse, 0.0), axis=0)
        return carry

    lax.fori_loop(0, heads, one_head, 0, unroll=True)


def local(first, heads, q, k, v):
    return pl.pallas_call(
        functools.partial(local_kernel, first, heads),
        out_shape=[
            jax.ShapeDtypeStruct((ROWS, heads * HEAD_DIM), F32),
            jax.ShapeDtypeStruct((heads, GROUPS, 8, 128), F32),
            jax.ShapeDtypeStruct((BLOCK, heads * HEAD_DIM), BF16),
        ],
        cost_estimate=cost(3 * 10**9, 3 * 2**20),
        compiler_params=params(),
        name="local_levels",
    )(order_matrix(), q, k, v)


def slab_lanes(x, copies):
    count = x.shape[0] // 8
    lane = lax.broadcasted_iota(jnp.int32, (count, 8, HEAD_DIM), 2)
    slab = lax.broadcasted_iota(jnp.int32, (count, 8, HEAD_DIM), 0)
    return jnp.sum(jnp.where(lane // copies == slab, x.reshape(count, 8, HEAD_DIM), 0.0), axis=0)


def of_head(h, refs):
    for heads, ref in zip(PORTIONS, refs):
        if h in heads:
            return ref, heads.index(h)


def third_kernel(near_ref, *refs):
    q3_refs, (att_ref, lse_ref) = refs[:-2], refs[-2:]
    cols = [slice(HEAD_DIM * h, HEAD_DIM * (h + 1)) for h in range(HEADS)]
    triples = []
    for h, col in enumerate(cols):
        ref, n = of_head(h, q3_refs)
        triples.append((ref[:, HEAD_DIM * n : HEAD_DIM * (n + 1)], near_ref[0:128, col], near_ref[128:256, col]))
    for h, (top, numer, denom) in enumerate(attend_all(triples)):
        att_ref[:, cols[h]] = numer / denom
        lse_ref[h] = slab_lanes(top + jnp.log2(denom) + 3.0, 1)


def third(near, q3s):
    return pl.pallas_call(
        third_kernel,
        out_shape=[jax.ShapeDtypeStruct((BLOCK, WIDTH), F32), jax.ShapeDtypeStruct((HEADS, 8, 128), F32)],
        cost_estimate=cost(10**8, 2**19),
        compiler_params=params(),
        name="third_level",
    )(near, *q3s)


def joined(one, other, col):
    return [jnp.concatenate([one[rows, col], other[rows, col]], axis=0) for rows in (slice(0, 64), slice(64, 128))]


def fronts_kernel(mine_ref, near_ref, out_ref):
    fronts = next_fronts(jnp.concatenate([mine_ref[...], near_ref[128:192]], axis=1))
    for i, x in enumerate(fronts):
        out_ref[BLOCK * i : BLOCK * i + 64] = x[:, :HALF]
        out_ref[BLOCK * i + 64 : BLOCK * (i + 1)] = x[:, HALF:]


def far_kernel(fronts_ref, *refs):
    fars, (att_ref, lse_ref) = refs[:-2], refs[-2:]
    across, diagonal, fifth_ref, across6, diagonal6 = fars
    cols = [slice(HEAD_DIM * h, HEAD_DIM * (h + 1)) for h in range(2)]
    triples = []
    for col in cols:
        pairs = [
            joined(across, diagonal, col),
            [fifth_ref[0:128, col], fifth_ref[128:256, col]],
            joined(across6, diagonal6, col),
        ]
        triples += [(fronts_ref[BLOCK * i : BLOCK * (i + 1), col], *pair) for i, pair in enumerate(pairs)]
    got = attend_all(triples)
    for h, col in enumerate(cols):
        parts = [(*got[3 * h + i], 4.0 + i) for i in range(3)]
        top, numer, denom = join(parts)
        att_ref[:, col] = numer / denom
        lse_ref[:, col] = top + jnp.log2(denom)


def far_levels(fronts, fars):
    return pl.pallas_call(
        far_kernel,
        out_shape=[
            jax.ShapeDtypeStruct((BLOCK, HALF), F32),
            jax.ShapeDtypeStruct((BLOCK, HALF), F32),
        ],
        cost_estimate=cost(5 * 10**8, 2**20),
        compiler_params=params(),
        name="far_levels",
    )(fronts, *fars)


def last_kernel(fronts_ref, near_ref, across_ref, diagonal_ref, att_ref, lse_ref, own_ref, send_ref):
    cols = [slice(HEAD_DIM * h, HEAD_DIM * (h + 1)) for h in range(2)]
    triples = []
    for col in cols:
        triples.append((fronts_ref[384:512, col], near_ref[0:128, col], near_ref[128:256, col]))
        triples.append((fronts_ref[512:640, col], *joined(across_ref, diagonal_ref, col)))
    got = attend_all(triples)
    for h, col in enumerate(cols):
        parts = [(*got[2 * h], 7.0), (*got[2 * h + 1], 8.0)]
        top, numer, denom = join([(lse_ref[:, col], att_ref[:, col], 1.0, 0.0)] + parts)
        att = numer / denom
        peak = top + jnp.log2(denom)
        own_ref[0:64, col] = att[:64]
        own_ref[64:72, col] = slab_lanes(peak[:64], 2)
        send_ref[0:64, col] = att[64:].astype(BF16)
        peak = slab_lanes(peak[64:], 2)
        high = peak.astype(BF16).astype(F32)
        middle = (peak - high).astype(BF16).astype(F32)
        low = (peak - high - middle).astype(BF16).astype(F32)
        row = high + pltpu.roll(middle, 16, 1) + pltpu.roll(low, 32, 1)
        send_ref[64:80, col] = jnp.concatenate([row, row], axis=0).astype(BF16)


def last_level(*args):
    return pl.pallas_call(
        last_kernel,
        out_shape=[jax.ShapeDtypeStruct((72, HALF), F32), jax.ShapeDtypeStruct((80, HALF), BF16)],
        cost_estimate=cost(2 * 10**8, 2**19),
        compiler_params=params(),
        name="last_levels",
    )(*args)


def merge_kernel(own_ref, got_ref, att3_ref, lse3_ref, *refs):
    out_ref, ss_ref, far = refs[-3:]
    count = len(PORTIONS)
    att_refs, lse_refs = refs[:count], refs[count : 2 * count]
    half = my_half()
    far[:, half_columns(half)] = own_ref[...]
    theirs = half_columns(1 - half)
    far[0:64, theirs] = got_ref[0:64].astype(F32)
    row = got_ref[64:80].astype(F32)[:8]
    for h in range(2):
        part = row[:, HEAD_DIM * h : HEAD_DIM * (h + 1)]
        part = part + pltpu.roll(part, 112, 1) + pltpu.roll(part, 96, 1)
        far[64:72, pl.ds(pl.multiple_of((1 - half) * HALF + HEAD_DIM * h, HEAD_DIM), HEAD_DIM)] = part
    lane = lax.broadcasted_iota(jnp.int32, (8, 128), 1)
    means, shares = [], []
    for h in range(HEADS):
        col = slice(HEAD_DIM * h, HEAD_DIM * (h + 1))
        peak, old = far[64:72, col], lse3_ref[h]
        share = 1.0 / (1.0 + jnp.exp2(peak - old))
        rows = []
        for n in range(16):
            mean = far[8 * (n // 2) : 8 * (n // 2 + 1), col]
            rows.append(mean + share[:, n : n + 1] * (att3_ref[8 * n : 8 * (n + 1), col] - mean))
        means.append(rows)
        most = jnp.maximum(peak, old)
        peak = most + jnp.log2(jnp.exp2(peak - most) + jnp.exp2(old - most))
        row = []
        for g in range(GROUPS):
            other = jnp.zeros((8, 128), F32)
            for i in range(4):
                other = jnp.where(lane // 8 == i, peak[:, 4 * g + i : 4 * g + i + 1], other)
            ref, n = of_head(h, lse_refs)
            row.append(1.0 / (1.0 + jnp.exp2(other - ref[n, g])))
        shares.append(row)
    ones = jnp.ones((HEAD_DIM, HEAD_DIM), BF16)
    squares = jnp.zeros((8, 128), F32)
    for g in range(GROUPS):
        totals = []
        for i in range(SLABS):
            rows = slice(GROUP * g + 8 * i, GROUP * g + 8 * (i + 1))
            total = None
            for h in range(HEADS):
                ref, n = of_head(h, att_refs)
                near = ref[rows, HEAD_DIM * n : HEAD_DIM * (n + 1)]
                mean = means[h][4 * g + i // 8]
                att = mean + shares[h][g][:, i : i + 1] * (near - mean)
                out_ref[rows, HEAD_DIM * h : HEAD_DIM * (h + 1)] = att
                total = att * att if total is None else total + att * att
            totals.append(total)
        total = jnp.concatenate(totals, axis=0)
        high = total.astype(BF16)
        low = (total - high.astype(F32)).astype(BF16)
        total = dot(high, ones) + dot(low, ones)
        for i in range(SLABS):
            squares = jnp.where(lane == g * SLABS + i, total[8 * i : 8 * (i + 1)], squares)
    ss_ref[...] = squares


def merge(*args):
    return pl.pallas_call(
        merge_kernel,
        out_shape=[jax.ShapeDtypeStruct((ROWS, WIDTH), F32), jax.ShapeDtypeStruct((8, 128), F32)],
        scratch_shapes=[pltpu.VMEM((72, WIDTH), F32)],
        cost_estimate=cost(10**8, 4 * 2**20),
        compiler_params=params(),
        name="merge",
    )(*args)


def finish_kernel(back_ref, ss_ref, gain_ref, att_ref, out_ref, held, sems):
    factor = lax.rsqrt(ss_ref[...] / FEAT + 1e-06)
    copies = []
    for g in range(GROUPS):
        pieces = []
        for i in range(SLABS):
            n = g * SLABS + i
            pieces.append(att_ref[8 * n : 8 * (n + 1), :] * factor[:, n : n + 1] * gain_ref[...])
        normed = jnp.concatenate(pieces, axis=0).astype(BF16)
        held[g] = dot(back_ref[...], normed).astype(BF16)
        copy = pltpu.make_async_copy(held.at[g], out_ref.at[pl.ds(GROUP * g, GROUP)], sems.at[g])
        copy.start()
        copies.append(copy)
    for copy in copies:
        copy.wait()


def finish(total, gain, att):
    return pl.pallas_call(
        finish_kernel,
        out_specs=pl.BlockSpec(memory_space=pl.ANY),
        out_shape=jax.ShapeDtypeStruct((ROWS, WIDTH), BF16),
        scratch_shapes=[pltpu.VMEM((GROUPS, GROUP, WIDTH), BF16), pltpu.SemaphoreType.DMA((GROUPS,))],
        cost_estimate=pl.CostEstimate(flops=3 * 10**8, bytes_accessed=3 * 2**20, transcendentals=0),
        compiler_params=pltpu.CompilerParams(vmem_limit_bytes=VMEM_LIMIT),
        name="finish",
    )(order_matrix().T, total, gain.reshape(1, WIDTH), att)


def after(args, *others):
    return lax.optimization_barrier((args, others))[0]


def body(queries, keys, values, norm_gain):
    count = lax.axis_size("ctx")

    def swap(x, mask):
        return lax.ppermute(x, "ctx", [(i, i ^ mask) for i in range(count)])

    def swap_heads(x, mask):
        return lax.ppermute(x, "head", [(i, i ^ mask) for i in range(lax.axis_size("head"))])

    def beside(portion, sent):
        heads = PORTIONS[portion]
        return local(heads[0], len(heads), *after((held_q, held_k, held_v), *sent))

    held_k, held_v, held_q, own3, own, diag, send, mine = coarse(keys, values, queries)
    near4 = swap(send, 1)
    across = swap(own, 2)
    diagonal = swap(diag, 3)
    got, (near4, across, diagonal) = lax.optimization_barrier((beside(0, (own, send)), (near4, across, diagonal)))
    locals_ = [got]
    own = small(fifth_kernel, "fifth_block", 2 * BLOCK, own, near4, across, diagonal)
    far5 = swap(own, 6)
    mine, near4 = after((mine, near4), own)
    fronts = small(fronts_kernel, "fronts", 5 * BLOCK, mine, near4)
    line6 = small(halve_kernel, "sixth_line", BLOCK, after(own, fronts))
    across6 = swap(line6, 8)
    diagonal6 = swap(line6, 14)
    near3 = swap(after(own3, line6), 1)
    got, (across6, diagonal6) = lax.optimization_barrier((beside(1, (line6,)), (across6, diagonal6)))
    locals_.append(got)
    own, last = blocks(seventh_kernel, "seventh_block", line6, far5, across6, diagonal6)
    near7 = swap(own, 16)
    across8 = swap(last, 32)
    diagonal8 = swap(last, 48)
    att6, lse6 = far_levels(after(fronts, last), [across, diagonal, far5, across6, diagonal6])
    kept, sent = last_level(fronts, near7, across8, diagonal8, att6, lse6)
    got = swap(sent, 1)
    att3, lse3 = third(near3, [x[2] for x in locals_])
    att, squares = merge(kept, got, att3, lse3, *[x[0] for x in locals_], *[x[1] for x in locals_])
    pair = swap_heads(squares, 2) + squares
    return finish(swap_heads(pair, 1) + pair, norm_gain, att)


def solution(mesh):
    return jax.shard_map(
        body,
        mesh=mesh,
        in_specs=(P("ctx", "head"), P("ctx", "head"), P("ctx", "head"), P("head")),
        out_specs=P("ctx", "head"),
        check_vma=False,
    )
```

```python
import functools
import math

import jax
import jax.numpy as jnp
import numpy as np
from jax import lax
from jax.experimental import pallas as pl
from jax.experimental.pallas import tpu as pltpu
from jax.sharding import PartitionSpec as P

HEAD_DIM = 128
BLOCK = 128
FEAT = 2048
HEADS = 4
ROWS = 1024
WIDTH = HEADS * HEAD_DIM
HALF = WIDTH // 2
GROUP = 256
GROUPS = ROWS // GROUP
SLABS = GROUP // 8
PORTIONS = ((0, 1), (2, 3))
SCALE = math.log2(math.e) / math.sqrt(HEAD_DIM)
BF16 = jnp.bfloat16
F32 = jnp.float32
VMEM_LIMIT = 48 * 1024 * 1024


def slab_order():
    token = np.arange(GROUP)
    return token // 128 * 128 + token % 16 * 8 + token // 16 % 8


def order_matrix():
    matrix = np.zeros((GROUP, GROUP), np.float32)
    matrix[slab_order(), np.arange(GROUP)] = 1.0
    return jnp.asarray(matrix, BF16)


def grid_of(rows, columns):
    row = lax.broadcasted_iota(jnp.int32, (rows, columns), 0)
    column = lax.broadcasted_iota(jnp.int32, (rows, columns), 1)
    return row, column


def halves(where):
    return jnp.where(where, 0.5, 0.0).astype(BF16)


def first_means():
    row, token = grid_of(GROUP // 2, GROUP)
    return halves(row == token // 128 * 64 + token % 16 // 2 * 8 + token // 16 % 8)


def pair_means(rows):
    row, column = grid_of(rows // 2, rows)
    return halves(column // 2 == row)


def spread_means(step):
    row, column = grid_of(64, 64)
    base = row // 2 ** (step + 1) * 2 ** (step + 1)
    return halves((column == base) | (column == base + 2**step))


def dot(a, b):
    return jnp.dot(a, b, preferred_element_type=F32)


def slab_means(x):
    rows, width = x.shape
    x = x.reshape(rows // 16, 2, 8, width)
    return ((x[:, 0] + x[:, 1]) * 0.5).reshape(rows // 2, width)


def rounded_slab_means(x):
    return slab_means(x.astype(F32)).astype(BF16)


def attend_all(triples):
    scores = [
        lax.dot_general(front, keyset, (((1,), (1,)), ((), ())), preferred_element_type=F32)
        for front, keyset, _ in triples
    ]
    tops = [jnp.max(s, axis=-1, keepdims=True) for s in scores]
    weights = [jnp.exp2((s - top) * SCALE).astype(BF16) for s, top in zip(scores, tops)]
    sums = [
        dot(w, jnp.concatenate([v, jnp.ones(v.shape, BF16)], axis=1)) for w, (_, _, v) in zip(weights, triples)
    ]
    return [
        (jnp.broadcast_to(top * SCALE, (top.shape[0], HEAD_DIM)), x[:, :HEAD_DIM], x[:, HEAD_DIM:])
        for top, x in zip(tops, sums)
    ]


def join(parts):
    top = functools.reduce(jnp.maximum, [part[0] for part in parts])
    numer = denom = None
    for (peak, n, d), level in parts_with(parts):
        factor = jnp.exp2(peak - top + level)
        numer = n * factor if numer is None else numer + n * factor
        denom = d * factor if denom is None else denom + d * factor
    return top, numer, denom


def parts_with(parts):
    return [(part[:3], part[3]) for part in parts]


def spread(x, copies):
    rows, width = x.shape
    x = jnp.broadcast_to(x.reshape(rows // 8, 1, 8, width), (rows // 8, copies, 8, width))
    return x.reshape(rows * copies, width)


def my_half():
    return lax.rem(lax.axis_index("ctx"), 2)


def half_columns(half):
    return pl.ds(pl.multiple_of(half * HALF, HALF), HALF)


def params(limit=VMEM_LIMIT):
    return pltpu.CompilerParams(vmem_limit_bytes=limit)


def cost(flops, bytes_accessed):
    return pl.CostEstimate(flops=flops, bytes_accessed=bytes_accessed, transcendentals=0)


def coarse_kernel(k_ref, v_ref, q_ref, held_k, held_v, held_q, third_ref, own_ref, diag_ref, send_ref, mine_ref, fourth, sems):
    sources = ((k_ref, held_k), (v_ref, held_v), (q_ref, held_q))
    copies = [pltpu.make_async_copy(ref, held, sems.at[i]) for i, (ref, held) in enumerate(sources)]
    for copy in copies:
        copy.start()
    means = first_means()
    for i, copy in enumerate(copies):
        copy.wait()
        held = sources[i][1]
        for g in range(GROUPS):
            x = dot(means, held[GROUP * g : GROUP * (g + 1), :]).astype(BF16)
            x = rounded_slab_means(rounded_slab_means(x))
            if i < 2:
                start = BLOCK * i + 32 * g
                third_ref[start : start + 32, :] = x
            start = 64 * i + 16 * g
            fourth[start : start + 16, :] = rounded_slab_means(x)
    half = my_half()
    mine, theirs = half_columns(half), half_columns(1 - half)
    own_ref[...] = fourth[0:128, mine]
    mine_ref[...] = fourth[128:192, mine]
    diag_ref[...] = fourth[0:128, theirs]
    send_ref[...] = fourth[:, theirs]


def coarse(k, v, q):
    return pl.pallas_call(
        coarse_kernel,
        in_specs=[pl.BlockSpec(memory_space=pl.ANY)] * 3,
        out_shape=[pltpu.VMEM((ROWS, WIDTH), BF16)] * 3
        + [pltpu.VMEM((2 * BLOCK, WIDTH), BF16)]
        + [pltpu.VMEM((BLOCK, HALF), BF16)] * 2
        + [pltpu.VMEM((192, HALF), BF16), pltpu.VMEM((64, HALF), BF16)],
        scratch_shapes=[pltpu.VMEM((192, WIDTH), BF16), pltpu.SemaphoreType.DMA((3,))],
        cost_estimate=cost(4 * 10**8, 3 * 2**20),
        compiler_params=params(),
        name="coarse",
    )(*[pltpu.with_memory_space_constraint(x, pltpu.HBM) for x in (k, v, q)])


def gather_means(out_ref, chunks):
    means = pair_means(BLOCK)
    for i, chunk in enumerate(chunks):
        x = dot(means, chunk).astype(BF16)
        out_ref[32 * i : 32 * (i + 1)] = x[:32]
        out_ref[BLOCK + 32 * i : BLOCK + 32 * (i + 1)] = x[32:]


def halve(ref):
    means = pair_means(BLOCK)
    return jnp.concatenate([dot(means, ref[BLOCK * i : BLOCK * (i + 1)]).astype(BF16) for i in range(2)], axis=0)


def fifth_kernel(*refs):
    gather_means(refs[-1], [ref[0:BLOCK] for ref in refs[:-1]])


def halve_kernel(x_ref, out_ref):
    out_ref[...] = halve(x_ref)


def small(kernel, name, rows, *args):
    return pl.pallas_call(
        kernel,
        out_shape=jax.ShapeDtypeStruct((rows, HALF), BF16),
        cost_estimate=cost(10**8, 2**18),
        compiler_params=params(),
        name=name,
    )(*args)


def seventh_kernel(line_ref, far_ref, across_ref, diagonal_ref, out_ref, next_ref):
    gather_means(out_ref, [line_ref[...], halve(far_ref), across_ref[...], diagonal_ref[...]])
    next_ref[...] = halve(out_ref)


def blocks(kernel, name, *chunks):
    return pl.pallas_call(
        kernel,
        out_shape=[jax.ShapeDtypeStruct((2 * BLOCK, HALF), BF16), jax.ShapeDtypeStruct((BLOCK, HALF), BF16)],
        cost_estimate=cost(10**8, 2**18),
        compiler_params=params(),
        name=name,
    )(*chunks)


def next_fronts(front):
    out = [front]
    for i in range(4):
        out.append(dot(spread_means(i), out[-1]).astype(BF16))
    return out


def local_kernel(first, heads, order_ref, q_ref, k_ref, v_ref, att_ref, lse_ref, q3_ref):
    lane = lax.broadcasted_iota(jnp.int32, (SLABS, 8, HEAD_DIM), 2)
    slab = lax.broadcasted_iota(jnp.int32, (SLABS, 8, HEAD_DIM), 0)
    groups = range(GROUPS)
    rows = [slice(GROUP * g, GROUP * (g + 1)) for g in groups]
    means = first_means()

    def one_head(h, carry):
        into = pl.ds(pl.multiple_of(h * HEAD_DIM, HEAD_DIM), HEAD_DIM)
        col = pl.ds(pl.multiple_of((h + first) * HEAD_DIM, HEAD_DIM), HEAD_DIM)
        q0, q1, q2, kv1, kv2 = [], [], [], [], []
        for g in groups:
            front = dot(order_ref[...], q_ref[rows[g], col])
            q0.append(front.astype(BF16))
            q1.append(slab_means(front).astype(BF16))
            q2.append(rounded_slab_means(q1[g]))
            both = jnp.concatenate([k_ref[rows[g], col], v_ref[rows[g], col]], axis=1)
            kv1.append(dot(means, both).astype(BF16))
            kv2.append(rounded_slab_means(kv1[g]))
        q3_ref[:, into] = rounded_slab_means(jnp.concatenate(q2, axis=0))
        far = [jnp.concatenate(kv2[2 - 2 * pair : 4 - 2 * pair], axis=0) for pair in range(2)]
        front = [jnp.concatenate(q2[2 * pair : 2 * pair + 2], axis=0) for pair in range(2)]
        triples = [(q, kv[:, :HEAD_DIM], kv[:, HEAD_DIM:]) for q, kv in zip(front, far)]
        for g in groups:
            far = kv1[g ^ 1]
            triples.append((q0[g], k_ref[rows[g], col], v_ref[rows[g], col]))
            triples.append((q1[g], far[:, :HEAD_DIM], far[:, HEAD_DIM:]))
        second = attend_all(triples)
        for g in groups:
            part0, part1 = second[2 * g + 2 : 2 * g + 4]
            half = slice(64 * (g % 2), 64 * (g % 2 + 1))
            part2 = [x[half] for x in second[g // 2]]
            top, numer, denom = join(
                [
                    (*part0, 0.0),
                    (*[spread(x, 2) for x in part1], 1.0),
                    (*[spread(x, 4) for x in part2], 2.0),
                ]
            )
            att_ref[rows[g], into] = numer / denom
            lse = (top + jnp.log2(denom)).reshape(SLABS, 8, HEAD_DIM)
            lse_ref[h, g] = jnp.sum(jnp.where(lane == slab, lse, 0.0), axis=0)
        return carry

    lax.fori_loop(0, heads, one_head, 0, unroll=True)


def local(first, heads, q, k, v):
    return pl.pallas_call(
        functools.partial(local_kernel, first, heads),
        out_shape=[
            jax.ShapeDtypeStruct((ROWS, heads * HEAD_DIM), F32),
            jax.ShapeDtypeStruct((heads, GROUPS, 8, 128), F32),
            jax.ShapeDtypeStruct((BLOCK, heads * HEAD_DIM), BF16),
        ],
        cost_estimate=cost(3 * 10**9, 3 * 2**20),
        compiler_params=params(),
        name="local_levels",
    )(order_matrix(), q, k, v)


def slab_lanes(x, copies):
    count = x.shape[0] // 8
    lane = lax.broadcasted_iota(jnp.int32, (count, 8, HEAD_DIM), 2)
    slab = lax.broadcasted_iota(jnp.int32, (count, 8, HEAD_DIM), 0)
    return jnp.sum(jnp.where(lane // copies == slab, x.reshape(count, 8, HEAD_DIM), 0.0), axis=0)


def of_head(h, refs):
    for heads, ref in zip(PORTIONS, refs):
        if h in heads:
            return ref, heads.index(h)


def third_kernel(near_ref, *refs):
    q3_refs, (att_ref, lse_ref) = refs[:-2], refs[-2:]
    cols = [slice(HEAD_DIM * h, HEAD_DIM * (h + 1)) for h in range(HEADS)]
    triples = []
    for h, col in enumerate(cols):
        ref, n = of_head(h, q3_refs)
        triples.append((ref[:, HEAD_DIM * n : HEAD_DIM * (n + 1)], near_ref[0:128, col], near_ref[128:256, col]))
    for h, (top, numer, denom) in enumerate(attend_all(triples)):
        att_ref[:, cols[h]] = numer / denom
        lse_ref[h] = slab_lanes(top + jnp.log2(denom) + 3.0, 1)


def third(near, q3s):
    return pl.pallas_call(
        third_kernel,
        out_shape=[jax.ShapeDtypeStruct((BLOCK, WIDTH), F32), jax.ShapeDtypeStruct((HEADS, 8, 128), F32)],
        cost_estimate=cost(10**8, 2**19),
        compiler_params=params(),
        name="third_level",
    )(near, *q3s)


def joined(one, other, col):
    return [jnp.concatenate([one[rows, col], other[rows, col]], axis=0) for rows in (slice(0, 64), slice(64, 128))]


def fronts_kernel(mine_ref, near_ref, out_ref):
    fronts = next_fronts(jnp.concatenate([mine_ref[...], near_ref[128:192]], axis=1))
    for i, x in enumerate(fronts):
        out_ref[BLOCK * i : BLOCK * i + 64] = x[:, :HALF]
        out_ref[BLOCK * i + 64 : BLOCK * (i + 1)] = x[:, HALF:]


def far_kernel(fronts_ref, *refs):
    fars, (att_ref, lse_ref) = refs[:-2], refs[-2:]
    across, diagonal, fifth_ref, across6, diagonal6 = fars
    cols = [slice(HEAD_DIM * h, HEAD_DIM * (h + 1)) for h in range(2)]
    triples = []
    for col in cols:
        pairs = [
            joined(across, diagonal, col),
            [fifth_ref[0:128, col], fifth_ref[128:256, col]],
            joined(across6, diagonal6, col),
        ]
        triples += [(fronts_ref[BLOCK * i : BLOCK * (i + 1), col], *pair) for i, pair in enumerate(pairs)]
    got = attend_all(triples)
    for h, col in enumerate(cols):
        parts = [(*got[3 * h + i], 4.0 + i) for i in range(3)]
        top, numer, denom = join(parts)
        att_ref[:, col] = numer / denom
        lse_ref[:, col] = top + jnp.log2(denom)


def far_levels(fronts, fars):
    return pl.pallas_call(
        far_kernel,
        out_shape=[
            jax.ShapeDtypeStruct((BLOCK, HALF), F32),
            jax.ShapeDtypeStruct((BLOCK, HALF), F32),
        ],
        cost_estimate=cost(5 * 10**8, 2**20),
        compiler_params=params(),
        name="far_levels",
    )(fronts, *fars)


def last_kernel(fronts_ref, near_ref, across_ref, diagonal_ref, att_ref, lse_ref, own_ref, send_ref):
    cols = [slice(HEAD_DIM * h, HEAD_DIM * (h + 1)) for h in range(2)]
    triples = []
    for col in cols:
        triples.append((fronts_ref[384:512, col], near_ref[0:128, col], near_ref[128:256, col]))
        triples.append((fronts_ref[512:640, col], *joined(across_ref, diagonal_ref, col)))
    got = attend_all(triples)
    for h, col in enumerate(cols):
        parts = [(*got[2 * h], 7.0), (*got[2 * h + 1], 8.0)]
        top, numer, denom = join([(lse_ref[:, col], att_ref[:, col], 1.0, 0.0)] + parts)
        att = numer / denom
        peak = top + jnp.log2(denom)
        own_ref[0:64, col] = att[:64]
        own_ref[64:72, col] = slab_lanes(peak[:64], 2)
        send_ref[0:64, col] = att[64:].astype(BF16)
        peak = slab_lanes(peak[64:], 2)
        high = peak.astype(BF16).astype(F32)
        middle = (peak - high).astype(BF16).astype(F32)
        low = (peak - high - middle).astype(BF16).astype(F32)
        row = high + pltpu.roll(middle, 16, 1) + pltpu.roll(low, 32, 1)
        send_ref[64:80, col] = jnp.concatenate([row, row], axis=0).astype(BF16)


def last_level(*args):
    return pl.pallas_call(
        last_kernel,
        out_shape=[jax.ShapeDtypeStruct((72, HALF), F32), jax.ShapeDtypeStruct((80, HALF), BF16)],
        cost_estimate=cost(2 * 10**8, 2**19),
        compiler_params=params(),
        name="last_levels",
    )(*args)


def merge_kernel(own_ref, got_ref, att3_ref, lse3_ref, *refs):
    out_ref, ss_ref, far = refs[-3:]
    count = len(PORTIONS)
    att_refs, lse_refs = refs[:count], refs[count : 2 * count]
    half = my_half()
    far[:, half_columns(half)] = own_ref[...]
    theirs = half_columns(1 - half)
    far[0:64, theirs] = got_ref[0:64].astype(F32)
    row = got_ref[64:80].astype(F32)[:8]
    for h in range(2):
        part = row[:, HEAD_DIM * h : HEAD_DIM * (h + 1)]
        part = part + pltpu.roll(part, 112, 1) + pltpu.roll(part, 96, 1)
        far[64:72, pl.ds(pl.multiple_of((1 - half) * HALF + HEAD_DIM * h, HEAD_DIM), HEAD_DIM)] = part
    lane = lax.broadcasted_iota(jnp.int32, (8, 128), 1)
    means, shares = [], []
    for h in range(HEADS):
        col = slice(HEAD_DIM * h, HEAD_DIM * (h + 1))
        peak, old = far[64:72, col], lse3_ref[h]
        share = 1.0 / (1.0 + jnp.exp2(peak - old))
        rows = []
        for n in range(16):
            mean = far[8 * (n // 2) : 8 * (n // 2 + 1), col]
            rows.append(mean + share[:, n : n + 1] * (att3_ref[8 * n : 8 * (n + 1), col] - mean))
        means.append(rows)
        most = jnp.maximum(peak, old)
        peak = most + jnp.log2(jnp.exp2(peak - most) + jnp.exp2(old - most))
        row = []
        for g in range(GROUPS):
            other = jnp.zeros((8, 128), F32)
            for i in range(4):
                other = jnp.where(lane // 8 == i, peak[:, 4 * g + i : 4 * g + i + 1], other)
            ref, n = of_head(h, lse_refs)
            row.append(1.0 / (1.0 + jnp.exp2(other - ref[n, g])))
        shares.append(row)
    ones = jnp.ones((HEAD_DIM, HEAD_DIM), BF16)
    squares = jnp.zeros((8, 128), F32)
    for g in range(GROUPS):
        totals = []
        for i in range(SLABS):
            rows = slice(GROUP * g + 8 * i, GROUP * g + 8 * (i + 1))
            total = None
            for h in range(HEADS):
                ref, n = of_head(h, att_refs)
                near = ref[rows, HEAD_DIM * n : HEAD_DIM * (n + 1)]
                mean = means[h][4 * g + i // 8]
                att = mean + shares[h][g][:, i : i + 1] * (near - mean)
                out_ref[rows, HEAD_DIM * h : HEAD_DIM * (h + 1)] = att
                total = att * att if total is None else total + att * att
            totals.append(total)
        total = jnp.concatenate(totals, axis=0)
        high = total.astype(BF16)
        low = (total - high.astype(F32)).astype(BF16)
        total = dot(high, ones) + dot(low, ones)
        for i in range(SLABS):
            squares = jnp.where(lane == g * SLABS + i, total[8 * i : 8 * (i + 1)], squares)
    ss_ref[...] = squares


def merge(*args):
    return pl.pallas_call(
        merge_kernel,
        out_shape=[jax.ShapeDtypeStruct((ROWS, WIDTH), F32), jax.ShapeDtypeStruct((8, 128), F32)],
        scratch_shapes=[pltpu.VMEM((72, WIDTH), F32)],
        cost_estimate=cost(10**8, 4 * 2**20),
        compiler_params=params(),
        name="merge",
    )(*args)


def finish_kernel(back_ref, ss_ref, gain_ref, att_ref, out_ref, held, sems):
    factor = lax.rsqrt(ss_ref[...] / FEAT + 1e-06)
    copies = []
    back = back_ref[0:BLOCK, 0:BLOCK]
    for g in range(ROWS // BLOCK):
        pieces = []
        for i in range(BLOCK // 8):
            n = g * (BLOCK // 8) + i
            pieces.append(att_ref[8 * n : 8 * (n + 1), :] * factor[:, n : n + 1] * gain_ref[...])
        normed = jnp.concatenate(pieces, axis=0).astype(BF16)
        held[g] = dot(back, normed).astype(BF16)
        copy = pltpu.make_async_copy(held.at[g], out_ref.at[pl.ds(BLOCK * g, BLOCK)], sems.at[g])
        copy.start()
        copies.append(copy)
    for copy in copies:
        copy.wait()


def finish(total, gain, att):
    return pl.pallas_call(
        finish_kernel,
        out_specs=pl.BlockSpec(memory_space=pl.ANY),
        out_shape=jax.ShapeDtypeStruct((ROWS, WIDTH), BF16),
        scratch_shapes=[pltpu.VMEM((ROWS // BLOCK, BLOCK, WIDTH), BF16), pltpu.SemaphoreType.DMA((ROWS // BLOCK,))],
        cost_estimate=pl.CostEstimate(flops=3 * 10**8, bytes_accessed=3 * 2**20, transcendentals=0),
        compiler_params=pltpu.CompilerParams(vmem_limit_bytes=VMEM_LIMIT),
        name="finish",
    )(order_matrix().T, total, gain.reshape(1, WIDTH), att)


def after(args, *others):
    return lax.optimization_barrier((args, others))[0]


def body(queries, keys, values, norm_gain):
    count = lax.axis_size("ctx")

    def swap(x, mask):
        return lax.ppermute(x, "ctx", [(i, i ^ mask) for i in range(count)])

    def swap_heads(x, mask):
        return lax.ppermute(x, "head", [(i, i ^ mask) for i in range(lax.axis_size("head"))])

    def beside(portion, sent):
        heads = PORTIONS[portion]
        return local(heads[0], len(heads), *after((held_q, held_k, held_v), *sent))

    held_k, held_v, held_q, own3, own, diag, send, mine = coarse(keys, values, queries)
    near4 = swap(send, 1)
    across = swap(own, 2)
    diagonal = swap(diag, 3)
    got, (near4, across, diagonal) = lax.optimization_barrier((beside(0, (own, send)), (near4, across, diagonal)))
    locals_ = [got]
    own = small(fifth_kernel, "fifth_block", 2 * BLOCK, own, near4, across, diagonal)
    far5 = swap(own, 6)
    mine, near4 = after((mine, near4), own)
    fronts = small(fronts_kernel, "fronts", 5 * BLOCK, mine, near4)
    line6 = small(halve_kernel, "sixth_line", BLOCK, after(own, fronts))
    across6 = swap(line6, 8)
    diagonal6 = swap(line6, 14)
    near3 = swap(after(own3, line6), 1)
    got, (across6, diagonal6) = lax.optimization_barrier((beside(1, (line6,)), (across6, diagonal6)))
    locals_.append(got)
    own, last = blocks(seventh_kernel, "seventh_block", line6, far5, across6, diagonal6)
    near7 = swap(own, 16)
    across8 = swap(last, 32)
    diagonal8 = swap(last, 48)
    att6, lse6 = far_levels(after(fronts, last), [across, diagonal, far5, across6, diagonal6])
    kept, sent = last_level(fronts, near7, across8, diagonal8, att6, lse6)
    got = swap(sent, 1)
    att3, lse3 = third(near3, [x[2] for x in locals_])
    att, squares = merge(kept, got, att3, lse3, *[x[0] for x in locals_], *[x[1] for x in locals_])
    pair = swap_heads(squares, 1) + squares
    return finish(swap_heads(pair, 2) + pair, norm_gain, att)


def solution(mesh):
    return jax.shard_map(
        body,
        mesh=mesh,
        in_specs=(P("ctx", "head"), P("ctx", "head"), P("ctx", "head"), P("head")),
        out_specs=P("ctx", "head"),
        check_vma=False,
    )
```
